32 devices in a mesh: blk: 8 (over y, x, core), grp: 4 (over z).
Axes of the slice: x: 2, y: 2, z: 4, core: 2. Of those that a mesh axis runs over, the one named last changes fastest.
Arguments:
- queries: float32 [4096, 1024], P(('blk', 'grp')), may hold values from -48 to 48
- passages: float32 [4096, 1024], P(('blk', 'grp')), may hold values from -48 to 48
- hard_table: bfloat16 [24576, 1024], P(('blk', 'grp')), may hold values from -12 to 12
- hard_index: int32 [4096, 8], P(('blk', 'grp')), may hold values from 0 to 3071, as said below
Outputs:
- mean_loss: float32 [], replicated
- query_grad: float32 [4096, 1024], P(('blk', 'grp'))
- passage_grad: float32 [4096, 1024], P(('blk', 'grp'))
- table_grad: bfloat16 [24576, 1024], P(('blk', 'grp'))
The draws below stay inside these ranges and needn't reach their ends.
Inputs may be any that keep to these rules, and one draw needn't show every extreme that they name: Owner o = hard_index // 768 is a batch group of the query's own loop shard. Among the 1024 entries of one device, the four owners are named exactly 384, 256, 256 and 128 times in some order, and the owner named 3 * 128 times is the same for all devices of one loop shard; entries may repeat.
All inputs are finite; a program needn't handle non-finite values.
Results may differ from the reference program's by a relative error of at most 0.0038.
Values may be sent and summed in bfloat16 or wider, within the bound.
A program may use at most 64 MiB of HBM per device.

```python
import math
import jax
import jax.numpy as jnp
from jax import lax

D = 1024
ROWS = 128
STOPS = 4
HARD = 8
HARD_DEV = 768
GROUPS = 4
BLOCKS = 8
BATCH = 4096
HARD_ROWS = 24576


def shared_pairs(key):
    base_key = jax.random.fold_in(key, 11)
    key_u, key_p, key_q, key_n = jax.random.split(base_key, 4)
    block_shape = (BLOCKS, GROUPS, ROWS, D)
    fresh = jnp.clip(jax.random.normal(key_u, block_shape, jnp.float32), -6.0, 6.0)
    noise_one = jnp.clip(jax.random.normal(key_n, (BATCH, D), jnp.float32), -6.0, 6.0)
    mixed = fresh + jnp.roll(fresh, -1, axis=0)
    mixed = mixed + jnp.roll(fresh, -2, axis=0)
    mixed = mixed + jnp.roll(fresh, -3, axis=0)
    direction = (0.5 * mixed).reshape(BATCH, D)
    own_dir = fresh.reshape(BATCH, D)
    device_total = BATCH // ROWS
    device_pos = (jnp.arange(BATCH) // ROWS).astype(jnp.float32) / (device_total - 1.0)
    align = (0.95 - 0.8 * device_pos)[:, None]
    spread = jnp.sqrt(1.0 - align * align)
    row_scale = jnp.exp(jax.random.uniform(key_p, (GROUPS, ROWS), jnp.float32, math.log(0.5), math.log(5.0)))
    pass_scale = jnp.broadcast_to(row_scale[None], (BLOCKS, GROUPS, ROWS)).reshape(BATCH, 1)
    level = jnp.exp(jax.random.uniform(key_q, (BATCH, 1), jnp.float32, math.log(0.8), math.log(1.6)))
    query_scale = level / pass_scale
    passage_vals = pass_scale * direction
    query_vals = query_scale * (align * own_dir + spread * noise_one)
    return (jnp.clip(query_vals, -48.0, 48.0), jnp.clip(passage_vals, -48.0, 48.0))


def draw_queries(key, part):
    return shared_pairs(key)[0]


def draw_passages(key, part):
    return shared_pairs(key)[1]


def draw_hard_index(key, part):
    device_count = BATCH // ROWS
    shard_count = device_count // GROUPS
    slot_keys = jax.random.split(jax.random.fold_in(key, 21), device_count)
    orders = jax.vmap(lambda each_key: jax.random.permutation(each_key, HARD * ROWS))(slot_keys)
    class_table = jnp.concatenate([jnp.zeros((3 * ROWS,), jnp.int32), jnp.ones((2 * ROWS,), jnp.int32), jnp.full((2 * ROWS,), 2, jnp.int32), jnp.full((ROWS,), 3, jnp.int32)])
    classes = class_table[orders]
    owner_keys = jax.random.split(jax.random.fold_in(key, 22), shard_count)
    owner_perm = jax.vmap(lambda each_key: jax.random.permutation(each_key, GROUPS))(owner_keys)
    shard_of_device = (jnp.arange(device_count) // GROUPS).astype(jnp.int32)
    device_perm = owner_perm[shard_of_device]
    owner_ids = jnp.take_along_axis(device_perm, classes, axis=1)
    row_ids = jax.random.randint(jax.random.fold_in(key, 23), (BATCH, HARD), 0, HARD_DEV, jnp.int32)
    return (owner_ids.reshape(BATCH, HARD) * HARD_DEV + row_ids).astype(jnp.int32)


def level_of(key, dims, pieces, least, largest):
    gain, own = 1.0, jax.random.fold_in(key, 6)
    for dim, parts in pieces:
        steps = jnp.exp(jax.random.uniform(jax.random.fold_in(own, dim), (parts,), jnp.float32, least / len(pieces), largest / len(pieces)))
        gain = gain * jnp.repeat(steps, dims[dim] // parts).reshape([-1 if axis == dim else 1 for axis in range(len(dims))])
    return gain


def normal_values(stream_key, shape, scale, most, cuts=(), kind=jnp.bfloat16):
    result = jax.random.normal(stream_key, shape, jnp.float32) * scale
    if len(cuts) > 0:
        result = level_of(stream_key, shape, cuts, -0.22, 0.18) * result
    return jnp.clip(result, min=-most, max=most).astype(kind)


def setup_inputs(seed: int = 0) -> dict:
    seeds = jax.random.split(jax.random.key(seed), 5)
    queries = draw_queries(jax.random.fold_in(seeds[4], 71), 0)
    passages = draw_passages(jax.random.fold_in(seeds[4], 71), 0)
    hard_table = normal_values(seeds[2], (HARD_ROWS, D), 2.0, 12.0, ((0, 32),))
    hard_index = draw_hard_index(jax.random.fold_in(seeds[4], 71), 0)
    return dict(queries=queries, passages=passages, hard_table=hard_table, hard_index=hard_index)


score_scale = 0.015625


def reference(queries, passages, hard_table, hard_index):
    query_split = queries.reshape(BLOCKS, GROUPS, ROWS, D)
    passage_split = passages.reshape(BLOCKS, GROUPS, ROWS, D)
    table_split = hard_table.reshape(BLOCKS, GROUPS * HARD_DEV, D)
    index_split = hard_index.reshape(BLOCKS, GROUPS, ROWS, HARD)
    highest = lax.Precision.HIGHEST

    def per_shard(shard):
        query_blk = query_split[shard]
        own_pass = passage_split[shard]
        window = jnp.stack([passage_split[(shard - stop_index) % BLOCKS] for stop_index in range(STOPS)])
        win_scores = jnp.einsum('grd,sgjd->grsj', query_blk, window, precision=highest) * score_scale
        hard_vecs = table_split[shard][index_split[shard]].astype(jnp.float32)
        hard_scores = jnp.einsum('grd,grkd->grk', query_blk, hard_vecs, precision=highest) * score_scale
        positive = jnp.sum(query_blk * own_pass, axis=-1) * score_scale
        joined = jnp.concatenate([win_scores.reshape(GROUPS, ROWS, STOPS * ROWS), hard_scores], axis=-1)
        top_val = jnp.max(joined, axis=-1)
        lse = top_val + jnp.log(jnp.sum(jnp.exp(joined - top_val[..., None]), axis=-1))
        loss_part = jnp.sum(lse - positive)
        weight = jnp.exp(win_scores - lse[:, :, None, None])
        hard_weight = jnp.exp(hard_scores - lse[..., None])
        grad_query = score_scale * (jnp.einsum('grsj,sgjd->grd', weight, window, precision=highest)
                                    + jnp.einsum('grk,grkd->grd', hard_weight, hard_vecs, precision=highest)
                                    - own_pass)
        grad_window = score_scale * jnp.einsum('grsj,grd->sgjd', weight, query_blk, precision=highest)
        grad_window = grad_window.at[0].add(-score_scale * query_blk)
        hard_term = (score_scale * hard_weight[..., None] * query_blk[:, :, None, :]).astype(jnp.bfloat16)
        hard_term = lax.optimization_barrier(hard_term).astype(jnp.float32)
        table_part = jnp.zeros((GROUPS * HARD_DEV, D), jnp.float32)
        table_part = table_part.at[index_split[shard].reshape(-1)].add(hard_term.reshape(-1, D))
        return loss_part, grad_query, grad_window, table_part

    loss_parts, grad_query, grad_window, table_parts = lax.map(per_shard, jnp.arange(BLOCKS, dtype=jnp.int32))
    grad_pass = jnp.zeros((BLOCKS, GROUPS, ROWS, D), jnp.float32)
    for stop_index in range(STOPS):
        grad_pass = grad_pass + jnp.roll(grad_window[:, stop_index], -stop_index, axis=0)
    mean_loss = jnp.sum(loss_parts) / BATCH
    return (mean_loss, grad_query.reshape(BATCH, D), grad_pass.reshape(BATCH, D),
            table_parts.reshape(HARD_ROWS, D).astype(jnp.bfloat16))
```

```python
import functools

import jax
import jax.numpy as jnp
from jax import lax
from jax.experimental import pallas as pl
from jax.experimental.pallas import tpu as pltpu
from jax.sharding import PartitionSpec as P

STOPS = 4
SCALE = 0.015625
TOP = 32766.0
LOW = -1e30
MESH = pl.DeviceIdType.MESH
HIGHEST = lax.Precision.HIGHEST

QUERY, QUERY_META, PASSAGE, PASSAGE_META, STATS, PARTIAL, LSE, GRAD = range(8)


def as_column(row, count):
    return jnp.broadcast_to(row, (128, count)).T[:, 0:1]


def as_row(column, count):
    return jnp.broadcast_to(column, (count, 128)).T[0:1, :]


def coded(value):
    largest = jnp.max(jnp.abs(value), axis=1, keepdims=True)
    largest = jnp.maximum(largest, 1e-30)
    code = jnp.round(value * (TOP / largest)).astype(jnp.int32).astype(jnp.int16)
    return code, largest * (1.0 / TOP)


def decoded(code):
    return code.astype(jnp.int32).astype(jnp.float32)


def nt(a, b, precision=None):
    return lax.dot_general(
        a, b, (((1,), (1,)), ((), ())), precision=precision, preferred_element_type=jnp.float32
    )


def kernel(
    loops, groups,
    q_ref, p_ref, t_ref, idx_ref,
    loss_ref, qg_ref, pg_ref, tg_ref,
    q16, qmeta, p16, pmeta, st_send, st_recv, a_send, a_recv, lse_send, lse_recv,
    g_send, g_recv, l_send, l_recv, sh, ch, sw, pf, qhi, qlo, whi,
    send_sem, recv_sem, lsend_sem, lrecv_sem,
):
    b = lax.axis_index("blk")
    g = lax.axis_index("grp")
    rows, width = q_ref.shape
    table_rows = t_ref.shape[0]
    barrier = pltpu.get_barrier_semaphore()
    for j in range(1, groups):
        pl.semaphore_signal(
            barrier, inc=1, device_id=(b, lax.rem(g + j, groups)), device_id_type=MESH
        )

    def greet(k, carry):
        pl.semaphore_signal(
            barrier, inc=1, device_id=(lax.rem(b + k, loops), g), device_id_type=MESH
        )
        return carry

    lax.fori_loop(1, loops, greet, 0)

    def copy(kind, j, src, dst, device):
        return pltpu.make_async_remote_copy(
            src_ref=src,
            dst_ref=dst,
            send_sem=send_sem.at[kind, j],
            recv_sem=recv_sem.at[kind, j],
            device_id=device,
            device_id_type=MESH,
        )

    def ahead(j):
        return (b, lax.rem(g + j, groups))

    def behind(j):
        return (b, lax.rem(g + groups - j, groups))

    copies = {}

    def go(kind, j, src, dst, device):
        copies[kind, j] = copy(kind, j, src, dst, device)
        copies[kind, j].start()

    query = q_ref[...]
    code, scale = coded(query)
    q16[0] = code
    qmeta[0, 0:8, :] = idx_ref[...]
    qmeta[0, 8:16, :] = jnp.broadcast_to(as_row(scale, rows), (8, rows))
    code, scale = coded(p_ref[...])
    p16[0] = code
    pmeta[0] = jnp.broadcast_to(as_row(scale, rows), (8, rows))

    pl.semaphore_wait(barrier, groups - 1 + loops - 1)
    for j in range(1, groups):
        go(QUERY_META, j, qmeta.at[0], qmeta.at[j], ahead(j))
    for s in range(1, STOPS):
        go(PASSAGE_META, s, pmeta.at[0], pmeta.at[s], (lax.rem(b + s, loops), g))
    for j in range(1, groups):
        go(QUERY, j, q16.at[0], q16.at[j], ahead(j))
    for s in range(1, STOPS):
        go(PASSAGE, s, p16.at[0], p16.at[s], (lax.rem(b + s, loops), g))

    row_id = lax.broadcasted_iota(jnp.int32, (table_rows, rows), 0).astype(jnp.float32) + (
        g * table_rows
    ).astype(jnp.float32)

    def hard_part(j):
        value = decoded(q16[j])
        high = value.astype(jnp.bfloat16)
        low = (value - high.astype(jnp.float32)).astype(jnp.bfloat16)
        qhi[j * rows:(j + 1) * rows, :] = high
        qlo[j * rows:(j + 1) * rows, :] = low
        table = t_ref[...]
        scores = (nt(table, high) + nt(table, low)) * (qmeta[j, 8:9, :] * SCALE)
        named = jnp.zeros((table_rows, rows), jnp.float32)
        for k in range(8):
            named = named + jnp.where(row_id == qmeta[j, k:k + 1, :], 1.0, 0.0)
        top = jnp.max(jnp.where(named > 0.0, scores, LOW), axis=0, keepdims=True)
        part = jnp.where(named > 0.0, named * jnp.exp(jnp.minimum(scores - top, 0.0)), 0.0)
        sh[j] = scores
        ch[j] = named
        st_send[j, 0:1, :] = top
        st_send[j, 1:2, :] = jnp.sum(part, axis=0, keepdims=True)
        if j > 0:
            go(STATS, j, st_send.at[j], st_recv.at[j], behind(j))
        partial = jnp.dot(
            part.T.astype(jnp.bfloat16), table, preferred_element_type=jnp.float32
        )
        a_send[j] = partial.astype(jnp.bfloat16)
        if j > 0:
            go(PARTIAL, j, a_send.at[j], a_recv.at[j], behind(j))

    def window_part(s):
        if s == 0:
            block = p_ref[...]
        else:
            block = decoded(p16[s]) * as_column(pmeta[s, 0:1, :], rows)
        pf[s * rows:(s + 1) * rows, :] = block
        sw[s * rows:(s + 1) * rows, :] = nt(block, query, HIGHEST) * SCALE

    st_send[...] = jnp.zeros_like(st_send)
    hard_part(0)
    window_part(0)
    positive = jnp.sum(query * p_ref[...]) * SCALE
    for s in range(1, STOPS):
        copies[PASSAGE_META, s].wait_recv()
        copies[PASSAGE, s].wait_recv()
        window_part(s)
    for j in range(1, groups):
        copies[QUERY_META, j].wait_recv()
        copies[QUERY, j].wait_recv()
        hard_part(j)

    window = sw[...]
    tops = [jnp.max(window, axis=0, keepdims=True), st_send[0, 0:1, :]]
    for j in range(1, groups):
        copies[STATS, j].wait_recv()
        tops.append(st_recv[j, 0:1, :])
    top = functools.reduce(jnp.maximum, tops)
    total = jnp.sum(jnp.exp(window - top), axis=0, keepdims=True)
    total = total + st_send[0, 1:2, :] * jnp.exp(tops[1] - top)
    for j in range(1, groups):
        total = total + st_recv[j, 1:2, :] * jnp.exp(tops[j + 1] - top)
    lse = top + jnp.log(total)
    lse_send[0:1, :] = lse
    lse_send[1:8, :] = jnp.broadcast_to(jnp.sum(lse) - positive, (7, rows))
    for j in range(1, groups):
        go(LSE, j, lse_send, lse_recv.at[j], ahead(j))

    weight = jnp.exp(window - lse)
    sw[...] = weight
    for s in range(STOPS - 1, 0, -1):
        term = jnp.dot(
            sw[s * rows:(s + 1) * rows, :], query,
            precision=HIGHEST, preferred_element_type=jnp.float32,
        )
        g_send[s] = term.astype(jnp.bfloat16)
        go(GRAD, s, g_send.at[s], g_recv.at[s], (lax.rem(b + loops - s, loops), g))

    group_loss = lse_send[1:2, :]
    whi[:, 0:rows] = (
        ch[0] * jnp.exp(jnp.minimum(sh[0] - lse, 0.0)) * (qmeta[0, 8:9, :] * SCALE)
    ).astype(jnp.bfloat16)
    for j in range(1, groups):
        copies[LSE, j].wait_recv()
        group_loss = group_loss + lse_recv[j, 1:2, :]
        whi[:, j * rows:(j + 1) * rows] = jnp.where(
            ch[j] > 0.0,
            ch[j] * jnp.exp(jnp.minimum(sh[j] - lse_recv[j, 0:1, :], 0.0)) * (qmeta[j, 8:9, :] * SCALE),
            0.0,
        ).astype(jnp.bfloat16)

    l_send[...] = jnp.broadcast_to(group_loss, (8, rows))
    l_recv[0] = jnp.broadcast_to(group_loss, (8, rows))

    def loss_copy(k):
        return pltpu.make_async_remote_copy(
            src_ref=l_send,
            dst_ref=l_recv.at[k],
            send_sem=lsend_sem.at[k],
            recv_sem=lrecv_sem.at[k],
            device_id=(lax.rem(b + k, loops), g),
            device_id_type=MESH,
        )

    def loss_start(k, carry):
        loss_copy(k).start()
        return carry

    lax.fori_loop(1, loops, loss_start, 0)

    tile = 256

    def table_tile(step, carry):
        cols = pl.ds(pl.multiple_of(step * tile, tile), tile)
        left = whi[...]
        tg_ref[:, cols] = (
            jnp.dot(left, qhi[:, cols], preferred_element_type=jnp.float32)
            + jnp.dot(left, qlo[:, cols], preferred_element_type=jnp.float32)
        ).astype(jnp.bfloat16)
        return carry

    lax.fori_loop(0, width // tile, table_tile, 0)

    qg_ref[...] = jnp.dot(
        sw[...].T, pf[...], precision=HIGHEST, preferred_element_type=jnp.float32
    )
    pg_ref[...] = jnp.dot(
        sw[0:rows, :], query, precision=HIGHEST, preferred_element_type=jnp.float32
    )

    parts = a_send[0].astype(jnp.float32) * as_column(jnp.exp(tops[1] - lse), rows)
    for j in range(1, groups):
        copies[PARTIAL, j].wait_recv()
        parts = parts + a_recv[j].astype(jnp.float32) * as_column(jnp.exp(tops[j + 1] - lse), rows)
    qg_ref[...] = (qg_ref[...] + parts - p_ref[...]) * SCALE
    sums = pg_ref[...]
    for s in range(1, STOPS):
        copies[GRAD, s].wait_recv()
        sums = sums + g_recv[s].astype(jnp.float32)
    pg_ref[...] = (sums - query) * SCALE

    def loss_wait(k, carry):
        loss_copy(k).wait()
        return carry

    lax.fori_loop(1, loops, loss_wait, 0)
    loss_ref[0, 0] = jnp.sum(l_recv[:, 0:1, 0:1]) / (rows * loops * groups)
    for each in copies.values():
        each.wait_send()


def local(loops, groups, queries, passages, hard_table, hard_index):
    rows, width = queries.shape
    table_rows = hard_table.shape[0]
    index = hard_index.T.astype(jnp.float32)
    vmem = pl.BlockSpec(memory_space=pltpu.VMEM)
    f32, bf16, i16 = jnp.float32, jnp.bfloat16, jnp.int16
    out = pl.pallas_call(
        functools.partial(kernel, loops, groups),
        out_shape=(
            jax.ShapeDtypeStruct((1, 1), f32),
            jax.ShapeDtypeStruct((rows, width), f32),
            jax.ShapeDtypeStruct((rows, width), f32),
            jax.ShapeDtypeStruct((table_rows, width), bf16),
        ),
        in_specs=[vmem] * 4,
        out_specs=(pl.BlockSpec(memory_space=pltpu.SMEM), vmem, vmem, vmem),
        scratch_shapes=[
            pltpu.VMEM((groups, rows, width), i16),
            pltpu.VMEM((groups, 16, rows), f32),
            pltpu.VMEM((STOPS, rows, width), i16),
            pltpu.VMEM((STOPS, 8, rows), f32),
            pltpu.VMEM((groups, 8, rows), f32),
            pltpu.VMEM((groups, 8, rows), f32),
            pltpu.VMEM((groups, rows, width), bf16),
            pltpu.VMEM((groups, rows, width), bf16),
            pltpu.VMEM((8, rows), f32),
            pltpu.VMEM((groups, 8, rows), f32),
            pltpu.VMEM((STOPS, rows, width), bf16),
            pltpu.VMEM((STOPS, rows, width), bf16),
            pltpu.VMEM((8, rows), f32),
            pltpu.VMEM((loops, 8, rows), f32),
            pltpu.VMEM((groups, table_rows, rows), f32),
            pltpu.VMEM((groups, table_rows, rows), f32),
            pltpu.VMEM((STOPS * rows, rows), f32),
            pltpu.VMEM((STOPS * rows, width), f32),
            pltpu.VMEM((groups * rows, width), bf16),
            pltpu.VMEM((groups * rows, width), bf16),
            pltpu.VMEM((table_rows, groups * rows), bf16),
            pltpu.SemaphoreType.DMA((8, max(groups, STOPS))),
            pltpu.SemaphoreType.DMA((8, max(groups, STOPS))),
            pltpu.SemaphoreType.DMA((loops,)),
            pltpu.SemaphoreType.DMA((loops,)),
        ],
        compiler_params=pltpu.CompilerParams(
            collective_id=0, has_side_effects=True, vmem_limit_bytes=48 * 1024 * 1024
        ),
    )(queries, passages, hard_table, index)
    return (out[0].reshape(()), out[1], out[2], out[3])


def solution(mesh):
    rows = P(("blk", "grp"), None)
    return jax.shard_map(
        functools.partial(local, mesh.shape["blk"], mesh.shape["grp"]),
        mesh=mesh,
        in_specs=(rows, rows, rows, rows),
        out_specs=(P(), rows, rows, rows),
        check_vma=False,
    )
```

```python
import functools

import jax
import jax.numpy as jnp
from jax import lax
from jax.experimental import pallas as pl
from jax.experimental.pallas import tpu as pltpu
from jax.sharding import PartitionSpec as P

STOPS = 4
SCALE = 0.015625
TOP = 32766.0
LOW = -1e30
MESH = pl.DeviceIdType.MESH
HIGHEST = lax.Precision.HIGHEST

QUERY, QUERY_META, PASSAGE, PASSAGE_META, STATS, PARTIAL, LSE, GRAD = range(8)


def as_column(row, count):
    return jnp.broadcast_to(row, (128, count)).T[:, 0:1]


def as_row(column, count):
    return jnp.broadcast_to(column, (count, 128)).T[0:1, :]


def coded(value):
    largest = jnp.max(jnp.abs(value), axis=1, keepdims=True)
    largest = jnp.maximum(largest, 1e-30)
    code = jnp.round(value * (TOP / largest)).astype(jnp.int32).astype(jnp.int16)
    return code, largest * (1.0 / TOP)


def decoded(code):
    return code.astype(jnp.int32).astype(jnp.float32)


def nt(a, b, precision=None):
    return lax.dot_general(
        a, b, (((1,), (1,)), ((), ())), precision=precision, preferred_element_type=jnp.float32
    )


def kernel(
    loops, groups,
    q_hbm, p_hbm, t_hbm, idx_ref,
    loss_ref, qg_ref, pg_ref, tg_ref,
    q_ref, p_ref, t_ref, q16, qmeta, p16, pmeta, st_send, st_recv, a_send, a_recv, lse_send, lse_recv,
    g_send, g_recv, l_send, l_recv, sh, ch, sw, pf, qhi, qlo, whi,
    send_sem, recv_sem, lsend_sem, lrecv_sem, load_sem,
):
    b = lax.axis_index("blk")
    g = lax.axis_index("grp")
    rows, width = q_ref.shape
    table_rows = t_ref.shape[0]
    loads = [
        pltpu.make_async_copy(src, dst, load_sem.at[i])
        for i, (src, dst) in enumerate(((q_hbm, q_ref), (p_hbm, p_ref), (t_hbm, t_ref)))
    ]
    for load in loads:
        load.start()
    barrier = pltpu.get_barrier_semaphore()
    for j in range(1, groups):
        pl.semaphore_signal(
            barrier, inc=1, device_id=(b, lax.rem(g + j, groups)), device_id_type=MESH
        )

    def greet(k, carry):
        pl.semaphore_signal(
            barrier, inc=1, device_id=(lax.rem(b + k, loops), g), device_id_type=MESH
        )
        return carry

    lax.fori_loop(1, loops, greet, 0)

    def copy(kind, j, src, dst, device, slot=None):
        return pltpu.make_async_remote_copy(
            src_ref=src,
            dst_ref=dst,
            send_sem=send_sem.at[kind, j],
            recv_sem=recv_sem.at[kind, j if slot is None else slot],
            device_id=device,
            device_id_type=MESH,
        )

    copies = {}

    def go(kind, j, src, dst, device, slot=None):
        copies[kind, j] = copy(kind, j, src, dst, device, slot)
        copies[kind, j].start()

    def arrived(kind, slot, ref):
        copy(kind, 0, ref, ref, (b, lax.rem(g + 1, groups)), slot).wait_recv()

    near = jnp.minimum(g, groups - 1 - g)
    right_longer = (g < groups - 1 - g).astype(jnp.int32)
    others = [None]
    for i in range(groups - 1):
        both = (i < 2 * near).astype(jnp.int32)
        distance = both * (i // 2 + 1) + (1 - both) * (i - near + 1)
        right = both * (i % 2) + (1 - both) * right_longer
        others.append(g + distance * (2 * right - 1))

    own_right = copy(QUERY, 0, q16.at[g], q16.at[g], (b, jnp.minimum(g + 1, groups - 1)), g)
    own_left = copy(QUERY, groups, q16.at[g], q16.at[g], (b, jnp.maximum(g - 1, 0)), g)

    def onward(j):
        src = others[j]
        step = jnp.where(src < g, 1, -1)
        dst = g + step
        return (dst >= 0) & (dst < groups), copy(
            QUERY, j, q16.at[src], q16.at[src], (b, jnp.clip(dst, 0, groups - 1)), src
        )

    def receive(j):
        src = others[j]
        arrived(QUERY, src, q16.at[src])
        valid, forward = onward(j)

        @pl.when(valid)
        def _():
            forward.start()

    loads[0].wait()
    query = q_ref[...]
    code, scale = coded(query)
    q16[g] = code
    qmeta[g, 0:8, :] = idx_ref[...]
    qmeta[g, 8:16, :] = jnp.broadcast_to(as_row(scale, rows), (8, rows))
    pl.semaphore_wait(barrier, groups - 1 + loops - 1)

    @pl.when(g < groups - 1)
    def _():
        own_right.start()

    @pl.when(g > 0)
    def _():
        own_left.start()

    for j in range(1, groups):
        go(QUERY_META, j, qmeta.at[g], qmeta.at[g], (b, others[j]), g)
    loads[1].wait()
    code, scale = coded(p_ref[...])
    p16[0] = code
    pmeta[0] = jnp.broadcast_to(as_row(scale, rows), (8, rows))
    for s in range(1, STOPS):
        go(PASSAGE_META, s, pmeta.at[0], pmeta.at[s], (lax.rem(b + s, loops), g))
    for s in range(1, STOPS):
        go(PASSAGE, s, p16.at[0], p16.at[s], (lax.rem(b + s, loops), g))
    loads[2].wait()

    row_id = lax.broadcasted_iota(jnp.int32, (table_rows, rows), 0).astype(jnp.float32) + (
        g * table_rows
    ).astype(jnp.float32)

    def hard_part(j):
        src = g if j == 0 else others[j]
        value = decoded(q16[src])
        high = value.astype(jnp.bfloat16)
        low = (value - high.astype(jnp.float32)).astype(jnp.bfloat16)
        qhi[j * rows:(j + 1) * rows, :] = high
        qlo[j * rows:(j + 1) * rows, :] = low
        table = t_ref[...]
        scores = (nt(table, high) + nt(table, low)) * (qmeta[src, 8:9, :] * SCALE)
        named = jnp.zeros((table_rows, rows), jnp.float32)
        for k in range(8):
            named = named + jnp.where(row_id == qmeta[src, k:k + 1, :], 1.0, 0.0)
        top = jnp.max(jnp.where(named > 0.0, scores, LOW), axis=0, keepdims=True)
        part = jnp.where(named > 0.0, named * jnp.exp(jnp.minimum(scores - top, 0.0)), 0.0)
        sh[j] = scores
        ch[j] = named
        st_send[j, 0:1, :] = top
        st_send[j, 1:2, :] = jnp.sum(part, axis=0, keepdims=True)
        if j > 0:
            go(STATS, j, st_send.at[j], st_recv.at[g], (b, src), g)
        partial = jnp.dot(
            part.T.astype(jnp.bfloat16), table, preferred_element_type=jnp.float32
        )
        a_send[j] = partial.astype(jnp.bfloat16)
        if j > 0:
            go(PARTIAL, j, a_send.at[j], a_recv.at[g], (b, src), g)

    def window_part(s):
        if s == 0:
            block = p_ref[...]
        else:
            block = decoded(p16[s]) * as_column(pmeta[s, 0:1, :], rows)
        pf[s * rows:(s + 1) * rows, :] = block
        sw[s * rows:(s + 1) * rows, :] = nt(block, query, HIGHEST) * SCALE

    st_send[...] = jnp.zeros_like(st_send)
    hard_part(0)
    window_part(0)
    positive = jnp.sum(query * p_ref[...]) * SCALE
    def window_next(s):
        copies[PASSAGE_META, s].wait_recv()
        copies[PASSAGE, s].wait_recv()
        window_part(s)

    receive(1)
    if groups > 2:

        @pl.when(near > 0)
        def _():
            receive(2)

    arrived(QUERY_META, others[1], qmeta.at[others[1]])
    hard_part(1)
    if groups > 2:

        @pl.when(near == 0)
        def _():
            receive(2)

    window_next(1)
    for j in range(2, groups):
        if j > 2:
            receive(j)
        arrived(QUERY_META, others[j], qmeta.at[others[j]])
        hard_part(j)
    for s in range(2, STOPS):
        window_next(s)

    window = sw[...]
    tops = [jnp.max(window, axis=0, keepdims=True), st_send[0, 0:1, :]]
    for j in range(1, groups):
        arrived(STATS, others[j], st_recv.at[others[j]])
        tops.append(st_recv[others[j], 0:1, :])
    top = functools.reduce(jnp.maximum, tops)
    total = jnp.sum(jnp.exp(window - top), axis=0, keepdims=True)
    total = total + st_send[0, 1:2, :] * jnp.exp(tops[1] - top)
    for j in range(1, groups):
        total = total + st_recv[others[j], 1:2, :] * jnp.exp(tops[j + 1] - top)
    lse = top + jnp.log(total)
    lse_send[0:1, :] = lse
    lse_send[1:8, :] = jnp.broadcast_to(jnp.sum(lse) - positive, (7, rows))
    for j in range(1, groups):
        go(LSE, j, lse_send, lse_recv.at[g], (b, others[j]), g)

    weight = jnp.exp(window - lse)
    sw[...] = weight
    for s in range(STOPS - 1, 0, -1):
        term = jnp.dot(
            sw[s * rows:(s + 1) * rows, :], query,
            precision=HIGHEST, preferred_element_type=jnp.float32,
        )
        g_send[s] = term.astype(jnp.bfloat16)
        go(GRAD, s, g_send.at[s], g_recv.at[s], (lax.rem(b + loops - s, loops), g))

    group_loss = lse_send[1:2, :]
    whi[:, 0:rows] = (
        ch[0] * jnp.exp(jnp.minimum(sh[0] - lse, 0.0)) * (qmeta[g, 8:9, :] * SCALE)
    ).astype(jnp.bfloat16)
    for j in range(1, groups):
        arrived(LSE, others[j], lse_recv.at[others[j]])
        group_loss = group_loss + lse_recv[others[j], 1:2, :]
        whi[:, j * rows:(j + 1) * rows] = jnp.where(
            ch[j] > 0.0,
            ch[j] * jnp.exp(jnp.minimum(sh[j] - lse_recv[others[j], 0:1, :], 0.0)) * (qmeta[others[j], 8:9, :] * SCALE),
            0.0,
        ).astype(jnp.bfloat16)

    l_send[...] = jnp.broadcast_to(group_loss, (8, rows))
    l_recv[0] = jnp.broadcast_to(group_loss, (8, rows))

    def loss_copy(k):
        return pltpu.make_async_remote_copy(
            src_ref=l_send,
            dst_ref=l_recv.at[k],
            send_sem=lsend_sem.at[k],
            recv_sem=lrecv_sem.at[k],
            device_id=(lax.rem(b + k, loops), g),
            device_id_type=MESH,
        )

    def loss_start(k, carry):
        loss_copy(k).start()
        return carry

    lax.fori_loop(1, loops, loss_start, 0)

    tile = 256

    def table_tile(step, carry):
        cols = pl.ds(pl.multiple_of(step * tile, tile), tile)
        left = whi[...]
        tg_ref[:, cols] = (
            jnp.dot(left, qhi[:, cols], preferred_element_type=jnp.float32)
            + jnp.dot(left, qlo[:, cols], preferred_element_type=jnp.float32)
        ).astype(jnp.bfloat16)
        return carry

    lax.fori_loop(0, width // tile, table_tile, 0)

    qg_ref[...] = jnp.dot(
        sw[...].T, pf[...], precision=HIGHEST, preferred_element_type=jnp.float32
    )
    pg_ref[...] = jnp.dot(
        sw[0:rows, :], query, precision=HIGHEST, preferred_element_type=jnp.float32
    )

    parts = a_send[0].astype(jnp.float32) * as_column(jnp.exp(tops[1] - lse), rows)
    for j in range(1, groups):
        arrived(PARTIAL, others[j], a_recv.at[others[j]])
        parts = parts + a_recv[others[j]].astype(jnp.float32) * as_column(jnp.exp(tops[j + 1] - lse), rows)
    qg_ref[...] = (qg_ref[...] + parts - p_ref[...]) * SCALE
    sums = pg_ref[...]
    for s in range(1, STOPS):
        copies[GRAD, s].wait_recv()
        sums = sums + g_recv[s].astype(jnp.float32)
    pg_ref[...] = (sums - query) * SCALE

    def loss_wait(k, carry):
        loss_copy(k).wait()
        return carry

    lax.fori_loop(1, loops, loss_wait, 0)
    loss_ref[0, 0] = jnp.sum(l_recv[:, 0:1, 0:1]) / (rows * loops * groups)
    for each in copies.values():
        each.wait_send()

    @pl.when(g < groups - 1)
    def _():
        own_right.wait_send()

    @pl.when(g > 0)
    def _():
        own_left.wait_send()

    for j in range(1, groups):
        valid, forward = onward(j)

        @pl.when(valid)
        def _():
            forward.wait_send()


def local(loops, groups, queries, passages, hard_table, hard_index):
    rows, width = queries.shape
    table_rows = hard_table.shape[0]
    index = hard_index.T.astype(jnp.float32)
    vmem = pl.BlockSpec(memory_space=pltpu.VMEM)
    f32, bf16, i16 = jnp.float32, jnp.bfloat16, jnp.int16
    out = pl.pallas_call(
        functools.partial(kernel, loops, groups),
        out_shape=(
            jax.ShapeDtypeStruct((1, 1), f32),
            jax.ShapeDtypeStruct((rows, width), f32),
            jax.ShapeDtypeStruct((rows, width), f32),
            jax.ShapeDtypeStruct((table_rows, width), bf16),
        ),
        in_specs=[pl.BlockSpec(memory_space=pl.ANY)] * 3 + [vmem],
        out_specs=(pl.BlockSpec(memory_space=pltpu.SMEM), vmem, vmem, vmem),
        scratch_shapes=[
            pltpu.VMEM((rows, width), f32),
            pltpu.VMEM((rows, width), f32),
            pltpu.VMEM((table_rows, width), bf16),
            pltpu.VMEM((groups, rows, width), i16),
            pltpu.VMEM((groups, 16, rows), f32),
            pltpu.VMEM((STOPS, rows, width), i16),
            pltpu.VMEM((STOPS, 8, rows), f32),
            pltpu.VMEM((groups, 8, rows), f32),
            pltpu.VMEM((groups, 8, rows), f32),
            pltpu.VMEM((groups, rows, width), bf16),
            pltpu.VMEM((groups, rows, width), bf16),
            pltpu.VMEM((8, rows), f32),
            pltpu.VMEM((groups, 8, rows), f32),
            pltpu.VMEM((STOPS, rows, width), bf16),
            pltpu.VMEM((STOPS, rows, width), bf16),
            pltpu.VMEM((8, rows), f32),
            pltpu.VMEM((loops, 8, rows), f32),
            pltpu.VMEM((groups, table_rows, rows), f32),
            pltpu.VMEM((groups, table_rows, rows), f32),
            pltpu.VMEM((STOPS * rows, rows), f32),
            pltpu.VMEM((STOPS * rows, width), f32),
            pltpu.VMEM((groups * rows, width), bf16),
            pltpu.VMEM((groups * rows, width), bf16),
            pltpu.VMEM((table_rows, groups * rows), bf16),
            pltpu.SemaphoreType.DMA((8, max(groups, STOPS) + 1)),
            pltpu.SemaphoreType.DMA((8, max(groups, STOPS) + 1)),
            pltpu.SemaphoreType.DMA((loops,)),
            pltpu.SemaphoreType.DMA((loops,)),
            pltpu.SemaphoreType.DMA((3,)),
        ],
        compiler_params=pltpu.CompilerParams(
            collective_id=0, has_side_effects=True, vmem_limit_bytes=60 * 1024 * 1024
        ),
    )(queries, passages, hard_table, index)
    return (out[0].reshape(()), out[1], out[2], out[3])


def solution(mesh):
    rows = P(("blk", "grp"), None)
    return jax.shard_map(
        functools.partial(local, mesh.shape["blk"], mesh.shape["grp"]),
        mesh=mesh,
        in_specs=(rows, rows, rows, rows),
        out_specs=(P(), rows, rows, rows),
        check_vma=False,
    )
```

```python
import functools

import jax
import jax.numpy as jnp
from jax import lax
from jax.experimental import pallas as pl
from jax.experimental.pallas import tpu as pltpu
from jax.sharding import PartitionSpec as P

STOPS = 4
SCALE = 0.015625
TOP = 32766.0
LOW = -1e30
MESH = pl.DeviceIdType.MESH
HIGHEST = lax.Precision.HIGHEST

QUERY, QUERY_META, PASSAGE, PASSAGE_META, STATS, PARTIAL, LSE, GRAD = range(8)


def as_column(row, count):
    return jnp.broadcast_to(row, (128, count)).T[:, 0:1]


def as_row(column, count):
    return jnp.broadcast_to(column, (count, 128)).T[0:1, :]


def coded(value):
    largest = jnp.max(jnp.abs(value), axis=1, keepdims=True)
    largest = jnp.maximum(largest, 1e-30)
    code = jnp.round(value * (TOP / largest)).astype(jnp.int32).astype(jnp.int16)
    return code, largest * (1.0 / TOP)


def halves(code):
    value = code.astype(jnp.int32).astype(jnp.float32)
    high = value.astype(jnp.bfloat16)
    return high, (value - high.astype(jnp.float32)).astype(jnp.bfloat16)


def two_terms(value):
    high = value.astype(jnp.bfloat16)
    return high, (value - high.astype(jnp.float32)).astype(jnp.bfloat16)


def mm(a, b):
    return jnp.dot(a, b, preferred_element_type=jnp.float32)


def nt(a, b, precision=None):
    return lax.dot_general(
        a, b, (((1,), (1,)), ((), ())), precision=precision, preferred_element_type=jnp.float32
    )


def kernel(
    loops, groups,
    q_hbm, p_hbm, t_hbm, idx_ref,
    loss_ref, qg_out, pg_out, tg_out,
    q_ref, p_ref, t_ref, qg_ref, pg_ref, tg_ref, q16, qmeta, p16, pmeta, st_send, st_recv, a_send, a_recv, lse_send, lse_recv,
    g_send, g_recv, l_send, l_recv, sh, ch, sw, phi, plo, gf, qhi, qlo, whi,
    send_sem, recv_sem, lsend_sem, lrecv_sem, load_sem, save_sem,
):
    b = lax.axis_index("blk")
    g = lax.axis_index("grp")
    rows, width = q_ref.shape
    table_rows = t_ref.shape[0]
    loads = [
        pltpu.make_async_copy(src, dst, load_sem.at[i])
        for i, (src, dst) in enumerate(((q_hbm, q_ref), (p_hbm, p_ref), (t_hbm, t_ref)))
    ]
    for load in loads:
        load.start()
    barrier = pltpu.get_barrier_semaphore()
    for j in range(1, groups):
        pl.semaphore_signal(
            barrier, inc=1, device_id=(b, lax.rem(g + j, groups)), device_id_type=MESH
        )

    def greet(k, carry):
        pl.semaphore_signal(
            barrier, inc=1, device_id=(lax.rem(b + k, loops), g), device_id_type=MESH
        )
        return carry

    lax.fori_loop(1, loops, greet, 0)

    def copy(kind, j, src, dst, device, slot=None):
        return pltpu.make_async_remote_copy(
            src_ref=src,
            dst_ref=dst,
            send_sem=send_sem.at[kind, j],
            recv_sem=recv_sem.at[kind, j if slot is None else slot],
            device_id=device,
            device_id_type=MESH,
        )

    copies = {}

    def go(kind, j, src, dst, device, slot=None):
        copies[kind, j] = copy(kind, j, src, dst, device, slot)
        copies[kind, j].start()

    def arrived(kind, slot, ref):
        copy(kind, 0, ref, ref, (b, lax.rem(g + 1, groups)), slot).wait_recv()

    near = jnp.minimum(g, groups - 1 - g)
    right_longer = (g < groups - 1 - g).astype(jnp.int32)
    others = [None]
    for i in range(groups - 1):
        both = (i < 2 * near).astype(jnp.int32)
        distance = both * (i // 2 + 1) + (1 - both) * (i - near + 1)
        right = both * (i % 2) + (1 - both) * right_longer
        others.append(g + distance * (2 * right - 1))

    own_right = copy(QUERY, 0, q16.at[g], q16.at[g], (b, jnp.minimum(g + 1, groups - 1)), g)
    own_left = copy(QUERY, groups, q16.at[g], q16.at[g], (b, jnp.maximum(g - 1, 0)), g)

    def onward(j):
        src = others[j]
        step = jnp.where(src < g, 1, -1)
        dst = g + step
        return (dst >= 0) & (dst < groups), copy(
            QUERY, j, q16.at[src], q16.at[src], (b, jnp.clip(dst, 0, groups - 1)), src
        )

    def receive(j):
        src = others[j]
        arrived(QUERY, src, q16.at[src])
        valid, forward = onward(j)

        @pl.when(valid)
        def _():
            forward.start()

    loads[0].wait()
    query = q_ref[...]
    code, scale = coded(query)
    q16[g] = code
    qmeta[g, 0:8, :] = idx_ref[...]
    qmeta[g, 8:16, :] = jnp.broadcast_to(as_row(scale, rows), (8, rows))
    pl.semaphore_wait(barrier, groups - 1 + loops - 1)

    @pl.when(g < groups - 1)
    def _():
        own_right.start()

    @pl.when(g > 0)
    def _():
        own_left.start()

    for j in range(1, groups):
        go(QUERY_META, j, qmeta.at[g], qmeta.at[g], (b, others[j]), g)
    loads[1].wait()
    code, scale = coded(p_ref[...])
    p16[0] = code
    pmeta[0] = jnp.broadcast_to(as_row(scale, rows), (8, rows))
    for s in range(1, STOPS):
        go(PASSAGE_META, s, pmeta.at[0], pmeta.at[s], (lax.rem(b + s, loops), g))
    for s in range(1, STOPS):
        go(PASSAGE, s, p16.at[0], p16.at[s], (lax.rem(b + s, loops), g))
    loads[2].wait()

    row_id = lax.broadcasted_iota(jnp.int32, (table_rows, rows), 0).astype(jnp.float32) + (
        g * table_rows
    ).astype(jnp.float32)

    def count(j):
        src = g if j == 0 else others[j]
        named = jnp.zeros((table_rows, rows), jnp.float32)
        for k in range(8):
            named = named + jnp.where(row_id == qmeta[src, k:k + 1, :], 1.0, 0.0)
        ch[j] = named

    def hard_part(j):
        src = g if j == 0 else others[j]
        high, low = halves(q16[src])
        qhi[j * rows:(j + 1) * rows, :] = high
        qlo[j * rows:(j + 1) * rows, :] = low
        table = t_ref[...]
        both = nt(table, jnp.concatenate([high, low], axis=0))
        scores = (both[:, 0:rows] + both[:, rows:]) * (qmeta[src, 8:9, :] * SCALE)
        named = ch[j]
        top = jnp.max(jnp.where(named > 0.0, scores, LOW), axis=0, keepdims=True)
        part = named * jnp.exp(jnp.minimum(scores - top, 0.0))
        sh[j] = scores
        st_send[j, 0:1, :] = top
        st_send[j, 1:2, :] = jnp.sum(part, axis=0, keepdims=True)
        if j > 0:
            go(STATS, j, st_send.at[j], st_recv.at[g], (b, src), g)
        a_send[j] = mm(part.T.astype(jnp.bfloat16), table).astype(jnp.bfloat16)
        if j > 0:
            go(PARTIAL, j, a_send.at[j], a_recv.at[g], (b, src), g)

    def window_part(s):
        if s == 0:
            sw[0:rows, :] = nt(p_ref[...], query, HIGHEST) * SCALE
            return
        high, low = halves(p16[s])
        at = slice((s - 1) * rows, s * rows)
        phi[at, :] = high
        plo[at, :] = low
        own_high, own_low = qhi[0:rows, :], qlo[0:rows, :]
        both = nt(high, jnp.concatenate([own_high, own_low], axis=0))
        scores = both[:, 0:rows] + both[:, rows:] + nt(low, own_high)
        sw[s * rows:(s + 1) * rows, :] = (
            scores * as_column(pmeta[s, 0:1, :], rows) * (qmeta[g, 8:9, :] * SCALE)
        )

    st_send[...] = jnp.zeros_like(st_send)
    count(0)
    hard_part(0)
    window_part(0)
    for j in range(1, groups):
        arrived(QUERY_META, others[j], qmeta.at[others[j]])
        count(j)
    positive = jnp.sum(query * p_ref[...]) * SCALE
    def window_next(s):
        copies[PASSAGE_META, s].wait_recv()
        copies[PASSAGE, s].wait_recv()
        window_part(s)

    receive(1)
    if groups > 2:

        @pl.when(near > 0)
        def _():
            receive(2)

    hard_part(1)
    if groups > 2:

        @pl.when(near == 0)
        def _():
            receive(2)

    window_next(1)
    for j in range(2, groups):
        if j > 2:
            receive(j)
        if j == groups - 1:
            for s in range(2, STOPS):
                window_next(s)
        hard_part(j)

    window = sw[...]
    tops = [jnp.max(window, axis=0, keepdims=True), st_send[0, 0:1, :]]
    for j in range(1, groups):
        arrived(STATS, others[j], st_recv.at[others[j]])
        tops.append(st_recv[others[j], 0:1, :])
    top = functools.reduce(jnp.maximum, tops)
    total = jnp.sum(jnp.exp(window - top), axis=0, keepdims=True)
    total = total + st_send[0, 1:2, :] * jnp.exp(tops[1] - top)
    for j in range(1, groups):
        total = total + st_recv[others[j], 1:2, :] * jnp.exp(tops[j + 1] - top)
    lse = top + jnp.log(total)
    lse_send[0:1, :] = lse
    lse_send[1:8, :] = jnp.broadcast_to(jnp.sum(lse) - positive, (7, rows))
    for j in range(1, groups):
        go(LSE, j, lse_send, lse_recv.at[g], (b, others[j]), g)

    sw[...] = jnp.exp(window - lse)
    whi_, wlo_ = two_terms(sw[rows:, :] * qmeta[g, 8:9, :])
    terms = mm(
        jnp.concatenate([whi_, whi_], axis=1),
        jnp.concatenate([qhi[0:rows, :], qlo[0:rows, :]], axis=0),
    ) + mm(wlo_, qhi[0:rows, :])
    odd = lax.rem(b, 2)
    partner = b + 1 - 2 * odd
    alone, joined = 3 - 2 * odd, 1 + 2 * odd
    for s in range(1, STOPS):
        term = terms[(s - 1) * rows:s * rows, :]
        gf[s - 1] = term
        g_send[s - 1] = term.astype(jnp.bfloat16)
    go(GRAD, 0, g_send.at[1], g_recv.at[0], (partner, g))
    go(GRAD, 1, g_send.at[alone - 1], g_recv.at[1], (lax.rem(b + loops - alone, loops), g))
    pg_ref[...] = jnp.dot(
        sw[0:rows, :], query, precision=HIGHEST, preferred_element_type=jnp.float32
    )

    group_loss = lse_send[1:2, :]
    whi[:, 0:rows] = (
        ch[0] * jnp.exp(jnp.minimum(sh[0] - lse, 0.0)) * (qmeta[g, 8:9, :] * SCALE)
    ).astype(jnp.bfloat16)
    for j in range(1, groups):
        arrived(LSE, others[j], lse_recv.at[others[j]])
        group_loss = group_loss + lse_recv[others[j], 1:2, :]
        whi[:, j * rows:(j + 1) * rows] = jnp.where(
            ch[j] > 0.0,
            ch[j] * jnp.exp(jnp.minimum(sh[j] - lse_recv[others[j], 0:1, :], 0.0)) * (qmeta[others[j], 8:9, :] * SCALE),
            0.0,
        ).astype(jnp.bfloat16)

    l_send[...] = jnp.broadcast_to(group_loss, (8, rows))
    l_recv[0] = jnp.broadcast_to(group_loss, (8, rows))

    def loss_copy(k):
        return pltpu.make_async_remote_copy(
            src_ref=l_send,
            dst_ref=l_recv.at[k],
            send_sem=lsend_sem.at[k],
            recv_sem=lrecv_sem.at[k],
            device_id=(lax.rem(b + k, loops), g),
            device_id_type=MESH,
        )

    def loss_start(k, carry):
        loss_copy(k).start()
        return carry

    lax.fori_loop(1, loops, loss_start, 0)

    copies[GRAD, 0].wait_recv()
    g_send[STOPS - 1] = (gf[joined - 1] + g_recv[0].astype(jnp.float32)).astype(jnp.bfloat16)
    go(GRAD, 2, g_send.at[STOPS - 1], g_recv.at[2], (lax.rem(b + loops - joined, loops), g))

    tile = 256

    def table_tile(step, carry):
        cols = pl.ds(pl.multiple_of(step * tile, tile), tile)
        left = whi[...]
        tg_ref[:, cols] = (
            jnp.dot(left, qhi[:, cols], preferred_element_type=jnp.float32)
            + jnp.dot(left, qlo[:, cols], preferred_element_type=jnp.float32)
        ).astype(jnp.bfloat16)
        return carry

    lax.fori_loop(0, width // tile, table_tile, 0)
    saves = [
        pltpu.make_async_copy(src, dst, save_sem.at[i])
        for i, (src, dst) in enumerate(((tg_ref, tg_out), (qg_ref, qg_out), (pg_ref, pg_out)))
    ]
    saves[0].start()

    whi_, wlo_ = two_terms(
        jnp.concatenate(
            [
                sw[s * rows:(s + 1) * rows, :] * as_column(pmeta[s, 0:1, :], rows)
                for s in range(1, STOPS)
            ],
            axis=0,
        ).T
    )
    qg_ref[...] = (
        jnp.dot(
            sw[0:rows, :].T, p_ref[...], precision=HIGHEST, preferred_element_type=jnp.float32
        )
        - p_ref[...]
        + (mm(whi_, phi[...]) + mm(wlo_, phi[...]) + mm(whi_, plo[...]))
    )

    parts = a_send[0].astype(jnp.float32) * as_column(jnp.exp(tops[1] - lse), rows)
    for j in range(1, groups):
        arrived(PARTIAL, others[j], a_recv.at[others[j]])
        parts = parts + a_recv[others[j]].astype(jnp.float32) * as_column(jnp.exp(tops[j + 1] - lse), rows)
    qg_ref[...] = (qg_ref[...] + parts) * SCALE
    saves[1].start()
    sums = pg_ref[...]
    for s in range(1, 3):
        copies[GRAD, s].wait_recv()
        sums = sums + g_recv[s].astype(jnp.float32)
    pg_ref[...] = (sums - query) * SCALE
    saves[2].start()

    def loss_wait(k, carry):
        loss_copy(k).wait()
        return carry

    lax.fori_loop(1, loops, loss_wait, 0)
    loss_ref[0, 0] = jnp.sum(l_recv[:, 0:1, 0:1]) / (rows * loops * groups)
    for each in copies.values():
        each.wait_send()

    @pl.when(g < groups - 1)
    def _():
        own_right.wait_send()

    @pl.when(g > 0)
    def _():
        own_left.wait_send()

    for j in range(1, groups):
        valid, forward = onward(j)

        @pl.when(valid)
        def _():
            forward.wait_send()

    for save in saves:
        save.wait()


def hand_over(a_ref, b_ref, c_ref, a_out, b_out, c_out, sem):
    moves = []
    for src, dst in ((a_ref, a_out), (b_ref, b_out), (c_ref, c_out)):
        part = src.shape[0] // 2
        for i in range(2):
            at = pl.ds(i * part, part)
            moves.append(pltpu.make_async_copy(src.at[at], dst.at[at], sem.at[len(moves)]))
    for move in moves:
        move.start()
    for move in moves:
        move.wait()


def local(loops, groups, queries, passages, hard_table, hard_index):
    rows, width = queries.shape
    table_rows = hard_table.shape[0]
    index = hard_index.T.astype(jnp.float32)
    anywhere = pl.BlockSpec(memory_space=pl.ANY)
    vmem = pl.BlockSpec(memory_space=pltpu.VMEM)
    f32, bf16, i16 = jnp.float32, jnp.bfloat16, jnp.int16
    out = pl.pallas_call(
        functools.partial(kernel, loops, groups),
        out_shape=(
            jax.ShapeDtypeStruct((1, 1), f32),
            jax.ShapeDtypeStruct((rows, width), f32),
            jax.ShapeDtypeStruct((rows, width), f32),
            jax.ShapeDtypeStruct((table_rows, width), bf16),
        ),
        in_specs=[anywhere] * 3 + [vmem],
        out_specs=(pl.BlockSpec(memory_space=pltpu.SMEM),) + (anywhere,) * 3,
        scratch_shapes=[
            pltpu.VMEM((rows, width), f32),
            pltpu.VMEM((rows, width), f32),
            pltpu.VMEM((table_rows, width), bf16),
            pltpu.VMEM((rows, width), f32),
            pltpu.VMEM((rows, width), f32),
            pltpu.VMEM((table_rows, width), bf16),
            pltpu.VMEM((groups, rows, width), i16),
            pltpu.VMEM((groups, 16, rows), f32),
            pltpu.VMEM((STOPS, rows, width), i16),
            pltpu.VMEM((STOPS, 8, rows), f32),
            pltpu.VMEM((groups, 8, rows), f32),
            pltpu.VMEM((groups, 8, rows), f32),
            pltpu.VMEM((groups, rows, width), bf16),
            pltpu.VMEM((groups, rows, width), bf16),
            pltpu.VMEM((8, rows), f32),
            pltpu.VMEM((groups, 8, rows), f32),
            pltpu.VMEM((STOPS, rows, width), bf16),
            pltpu.VMEM((STOPS, rows, width), bf16),
            pltpu.VMEM((8, rows), f32),
            pltpu.VMEM((loops, 8, rows), f32),
            pltpu.VMEM((groups, table_rows, rows), f32),
            pltpu.VMEM((groups, table_rows, rows), f32),
            pltpu.VMEM((STOPS * rows, rows), f32),
            pltpu.VMEM(((STOPS - 1) * rows, width), bf16),
            pltpu.VMEM(((STOPS - 1) * rows, width), bf16),
            pltpu.VMEM((STOPS - 1, rows, width), f32),
            pltpu.VMEM((groups * rows, width), bf16),
            pltpu.VMEM((groups * rows, width), bf16),
            pltpu.VMEM((table_rows, groups * rows), bf16),
            pltpu.SemaphoreType.DMA((8, max(groups, STOPS) + 1)),
            pltpu.SemaphoreType.DMA((8, max(groups, STOPS) + 1)),
            pltpu.SemaphoreType.DMA((loops,)),
            pltpu.SemaphoreType.DMA((loops,)),
            pltpu.SemaphoreType.DMA((3,)),
            pltpu.SemaphoreType.DMA((3,)),
        ],
        compiler_params=pltpu.CompilerParams(
            collective_id=0, has_side_effects=True, vmem_limit_bytes=60 * 1024 * 1024
        ),
    )(queries, passages, hard_table, index)
    done = pl.pallas_call(
        hand_over,
        out_shape=tuple(jax.ShapeDtypeStruct(x.shape, x.dtype) for x in out[1:]),
        in_specs=[anywhere] * 3,
        out_specs=(anywhere,) * 3,
        scratch_shapes=[pltpu.SemaphoreType.DMA((6,))],
        compiler_params=pltpu.CompilerParams(vmem_limit_bytes=60 * 1024 * 1024),
    )(*out[1:])
    return (out[0].reshape(()),) + tuple(done)


def solution(mesh):
    rows = P(("blk", "grp"), None)
    return jax.shard_map(
        functools.partial(local, mesh.shape["blk"], mesh.shape["grp"]),
        mesh=mesh,
        in_specs=(rows, rows, rows, rows),
        out_specs=(P(), rows, rows, rows),
        check_vma=False,
    )
```

```python
import functools

import jax
import jax.numpy as jnp
from jax import lax
from jax.experimental import pallas as pl
from jax.experimental.pallas import tpu as pltpu
from jax.sharding import PartitionSpec as P

STOPS = 4
SCALE = 0.015625
TOP = 32766.0
LOW = -1e30
MESH = pl.DeviceIdType.MESH
HIGHEST = lax.Precision.HIGHEST

QUERY, QUERY_META, PASSAGE, PASSAGE_META, STATS, PARTIAL, LSE, GRAD = range(8)


def as_column(row, count):
    return jnp.broadcast_to(row, (128, count)).T[:, 0:1]


def as_row(column, count):
    return jnp.broadcast_to(column, (count, 128)).T[0:1, :]


def coded(value):
    largest = jnp.max(jnp.abs(value), axis=1, keepdims=True)
    largest = jnp.maximum(largest, 1e-30)
    code = jnp.round(value * (TOP / largest)).astype(jnp.int32).astype(jnp.int16)
    return code, largest * (1.0 / TOP)


def halves(code):
    value = code.astype(jnp.int32).astype(jnp.float32)
    high = value.astype(jnp.bfloat16)
    return high, (value - high.astype(jnp.float32)).astype(jnp.bfloat16)


def two_terms(value):
    high = value.astype(jnp.bfloat16)
    return high, (value - high.astype(jnp.float32)).astype(jnp.bfloat16)


def mm(a, b):
    return jnp.dot(a, b, preferred_element_type=jnp.float32)


def nt(a, b, precision=None):
    return lax.dot_general(
        a, b, (((1,), (1,)), ((), ())), precision=precision, preferred_element_type=jnp.float32
    )


def kernel(
    loops, groups,
    q_hbm, p_hbm, t_hbm, idx_ref,
    loss_ref, qg_out, pg_out, tg_out,
    q_ref, p_ref, t_ref, qg_ref, pg_ref, tg_ref, q16, qmeta, p16, pmeta, st_send, st_recv, a_send, a_recv, lse_send, lse_recv,
    g_send, g_recv, l_send, l_recv, sh, ch, sw, phi, plo, gf, qhi, qlo, whi,
    send_sem, recv_sem, lsend_sem, lrecv_sem, load_sem, save_sem,
):
    b = lax.axis_index("blk")
    g = lax.axis_index("grp")
    rows, width = q_ref.shape
    table_rows = t_ref.shape[0]
    loads = [
        pltpu.make_async_copy(src, dst, load_sem.at[i])
        for i, (src, dst) in enumerate(((q_hbm, q_ref), (p_hbm, p_ref), (t_hbm, t_ref)))
    ]
    for load in loads:
        load.start()
    barrier = pltpu.get_barrier_semaphore()
    for j in range(1, groups):
        pl.semaphore_signal(
            barrier, inc=1, device_id=(b, lax.rem(g + j, groups)), device_id_type=MESH
        )

    def greet(k, carry):
        pl.semaphore_signal(
            barrier, inc=1, device_id=(lax.rem(b + k, loops), g), device_id_type=MESH
        )
        return carry

    lax.fori_loop(1, loops, greet, 0)

    def copy(kind, j, src, dst, device, slot=None):
        return pltpu.make_async_remote_copy(
            src_ref=src,
            dst_ref=dst,
            send_sem=send_sem.at[kind, j],
            recv_sem=recv_sem.at[kind, j if slot is None else slot],
            device_id=device,
            device_id_type=MESH,
        )

    copies = {}

    def go(kind, j, src, dst, device, slot=None):
        copies[kind, j] = copy(kind, j, src, dst, device, slot)
        copies[kind, j].start()

    def arrived(kind, slot, ref):
        copy(kind, 0, ref, ref, (b, lax.rem(g + 1, groups)), slot).wait_recv()

    near = jnp.minimum(g, groups - 1 - g)
    right_longer = (g < groups - 1 - g).astype(jnp.int32)
    others = [None]
    for i in range(groups - 1):
        both = (i < 2 * near).astype(jnp.int32)
        distance = both * (i // 2 + 1) + (1 - both) * (i - near + 1)
        right = both * (i % 2) + (1 - both) * right_longer
        others.append(g + distance * (2 * right - 1))

    own_right = copy(QUERY, 0, q16.at[g], q16.at[g], (b, jnp.minimum(g + 1, groups - 1)), g)
    own_left = copy(QUERY, groups, q16.at[g], q16.at[g], (b, jnp.maximum(g - 1, 0)), g)

    def onward(j):
        src = others[j]
        step = jnp.where(src < g, 1, -1)
        dst = g + step
        return (dst >= 0) & (dst < groups), copy(
            QUERY, j, q16.at[src], q16.at[src], (b, jnp.clip(dst, 0, groups - 1)), src
        )

    def receive(j):
        src = others[j]
        arrived(QUERY, src, q16.at[src])
        valid, forward = onward(j)

        @pl.when(valid)
        def _():
            forward.start()

    loads[0].wait()
    query = q_ref[...]
    code, scale = coded(query)
    q16[g] = code
    qmeta[g, 0:8, :] = idx_ref[...].astype(jnp.float32)
    qmeta[g, 8:16, :] = jnp.broadcast_to(as_row(scale, rows), (8, rows))
    pl.semaphore_wait(barrier, groups - 1 + loops - 1)

    @pl.when(g < groups - 1)
    def _():
        own_right.start()

    @pl.when(g > 0)
    def _():
        own_left.start()

    for j in range(1, groups):
        go(QUERY_META, j, qmeta.at[g], qmeta.at[g], (b, others[j]), g)
    loads[1].wait()
    code, scale = coded(p_ref[...])
    p16[0] = code
    pmeta[0] = jnp.broadcast_to(as_row(scale, rows), (8, rows))
    for s in range(1, STOPS):
        go(PASSAGE_META, s, pmeta.at[0], pmeta.at[s], (lax.rem(b + s, loops), g))
    for s in (3, 1):
        go(PASSAGE, s, p16.at[0], p16.at[s], (lax.rem(b + s, loops), g))
    loads[2].wait()

    row_id = lax.broadcasted_iota(jnp.int32, (table_rows, rows), 0).astype(jnp.float32) + (
        g * table_rows
    ).astype(jnp.float32)

    def count(j):
        src = g if j == 0 else others[j]
        named = jnp.zeros((table_rows, rows), jnp.float32)
        for k in range(8):
            named = named + jnp.where(row_id == qmeta[src, k:k + 1, :], 1.0, 0.0)
        ch[j] = named

    def hard_part(j):
        src = g if j == 0 else others[j]
        high, low = halves(q16[src])
        qhi[j * rows:(j + 1) * rows, :] = high
        qlo[j * rows:(j + 1) * rows, :] = low
        table = t_ref[...]
        both = nt(table, jnp.concatenate([high, low], axis=0))
        scores = (both[:, 0:rows] + both[:, rows:]) * (qmeta[src, 8:9, :] * SCALE)
        named = ch[j]
        top = jnp.max(jnp.where(named > 0.0, scores, LOW), axis=0, keepdims=True)
        part = named * jnp.exp(jnp.minimum(scores - top, 0.0))
        sh[j] = scores
        st_send[j, 0:1, :] = top
        st_send[j, 1:2, :] = jnp.sum(part, axis=0, keepdims=True)
        if j > 0:
            go(STATS, j, st_send.at[j], st_recv.at[g], (b, src), g)
        a_send[j] = mm(part.T.astype(jnp.bfloat16), table).astype(jnp.bfloat16)
        if j > 0:
            go(PARTIAL, j, a_send.at[j], a_recv.at[g], (b, src), g)

    def window_part(s):
        if s == 0:
            sw[0:rows, :] = nt(p_ref[...], query, HIGHEST) * SCALE
            return
        high, low = halves(p16[s])
        at = slice((s - 1) * rows, s * rows)
        phi[at, :] = high
        plo[at, :] = low
        own_high, own_low = qhi[0:rows, :], qlo[0:rows, :]
        both = nt(high, jnp.concatenate([own_high, own_low], axis=0))
        scores = both[:, 0:rows] + both[:, rows:] + nt(low, own_high)
        sw[s * rows:(s + 1) * rows, :] = (
            scores * as_column(pmeta[s, 0:1, :], rows) * (qmeta[g, 8:9, :] * SCALE)
        )

    st_send[...] = jnp.zeros_like(st_send)
    count(0)
    hard_part(0)
    window_part(0)
    for j in range(1, groups):
        arrived(QUERY_META, others[j], qmeta.at[others[j]])
        count(j)
    positive = jnp.sum(query * p_ref[...]) * SCALE
    def window_next(s):
        copies[PASSAGE_META, s].wait_recv()
        if s == 2:
            copies[PASSAGE, s].wait_recv()
        window_part(s)

    receive(1)
    if groups > 2:

        @pl.when(near > 0)
        def _():
            receive(2)

    hard_part(1)
    if groups > 2:

        @pl.when(near == 0)
        def _():
            receive(2)

    odd = lax.rem(b, 2)
    partner = b + 1 - 2 * odd
    for s in (1, 3):
        copies[PASSAGE, s].wait_recv()
    go(PASSAGE, 2, p16.at[1 + 2 * odd], p16.at[2], (partner, g))
    window_next(1)
    for j in range(2, groups):
        if j > 2:
            receive(j)
        if j == groups - 1:
            for s in range(2, STOPS):
                window_next(s)
        hard_part(j)

    window = sw[...]
    tops = [jnp.max(window, axis=0, keepdims=True), st_send[0, 0:1, :]]
    for j in range(1, groups):
        arrived(STATS, others[j], st_recv.at[others[j]])
        tops.append(st_recv[others[j], 0:1, :])
    top = functools.reduce(jnp.maximum, tops)
    total = jnp.sum(jnp.exp(window - top), axis=0, keepdims=True)
    total = total + st_send[0, 1:2, :] * jnp.exp(tops[1] - top)
    for j in range(1, groups):
        total = total + st_recv[others[j], 1:2, :] * jnp.exp(tops[j + 1] - top)
    lse = top + jnp.log(total)
    lse_send[0:1, :] = lse
    lse_send[1:8, :] = jnp.broadcast_to(jnp.sum(lse) - positive, (7, rows))
    for j in range(1, groups):
        go(LSE, j, lse_send, lse_recv.at[g], (b, others[j]), g)

    sw[...] = jnp.exp(window - lse)
    whi_, wlo_ = two_terms(sw[rows:, :] * qmeta[g, 8:9, :])
    terms = mm(
        jnp.concatenate([whi_, whi_], axis=1),
        jnp.concatenate([qhi[0:rows, :], qlo[0:rows, :]], axis=0),
    ) + mm(wlo_, qhi[0:rows, :])
    alone, joined = 3 - 2 * odd, 1 + 2 * odd
    for s in range(1, STOPS):
        term = terms[(s - 1) * rows:s * rows, :]
        gf[s - 1] = term
        g_send[s - 1] = term.astype(jnp.bfloat16)
    go(GRAD, 0, g_send.at[1], g_recv.at[0], (partner, g))
    go(GRAD, 1, g_send.at[alone - 1], g_recv.at[1], (lax.rem(b + loops - alone, loops), g))
    pg_ref[...] = jnp.dot(
        sw[0:rows, :], query, precision=HIGHEST, preferred_element_type=jnp.float32
    )

    group_loss = lse_send[1:2, :]
    whi[:, 0:rows] = (
        ch[0] * jnp.exp(jnp.minimum(sh[0] - lse, 0.0)) * (qmeta[g, 8:9, :] * SCALE)
    ).astype(jnp.bfloat16)
    for j in range(1, groups):
        arrived(LSE, others[j], lse_recv.at[others[j]])
        group_loss = group_loss + lse_recv[others[j], 1:2, :]
        whi[:, j * rows:(j + 1) * rows] = jnp.where(
            ch[j] > 0.0,
            ch[j] * jnp.exp(jnp.minimum(sh[j] - lse_recv[others[j], 0:1, :], 0.0)) * (qmeta[others[j], 8:9, :] * SCALE),
            0.0,
        ).astype(jnp.bfloat16)

    l_send[...] = jnp.broadcast_to(group_loss, (8, rows))
    l_recv[0] = jnp.broadcast_to(group_loss, (8, rows))

    def loss_copy(k):
        return pltpu.make_async_remote_copy(
            src_ref=l_send,
            dst_ref=l_recv.at[k],
            send_sem=lsend_sem.at[k],
            recv_sem=lrecv_sem.at[k],
            device_id=(lax.rem(b + k, loops), g),
            device_id_type=MESH,
        )

    def loss_start(k, carry):
        loss_copy(k).start()
        return carry

    lax.fori_loop(1, loops, loss_start, 0)

    copies[GRAD, 0].wait_recv()
    g_send[STOPS - 1] = (gf[joined - 1] + g_recv[0].astype(jnp.float32)).astype(jnp.bfloat16)
    go(GRAD, 2, g_send.at[STOPS - 1], g_recv.at[2], (lax.rem(b + loops - joined, loops), g))

    tile = 256

    def table_tile(step, carry):
        cols = pl.ds(pl.multiple_of(step * tile, tile), tile)
        left = whi[...]
        tg_ref[:, cols] = (
            jnp.dot(left, qhi[:, cols], preferred_element_type=jnp.float32)
            + jnp.dot(left, qlo[:, cols], preferred_element_type=jnp.float32)
        ).astype(jnp.bfloat16)
        return carry

    lax.fori_loop(0, width // tile, table_tile, 0)
    saves = [
        pltpu.make_async_copy(src, dst, save_sem.at[i])
        for i, (src, dst) in enumerate(((tg_ref, tg_out), (qg_ref, qg_out), (pg_ref, pg_out)))
    ]
    saves[0].start()

    whi_, wlo_ = two_terms(
        jnp.concatenate(
            [
                sw[s * rows:(s + 1) * rows, :] * as_column(pmeta[s, 0:1, :], rows)
                for s in range(1, STOPS)
            ],
            axis=0,
        ).T
    )
    qg_ref[...] = (
        jnp.dot(
            sw[0:rows, :].T, p_ref[...], precision=HIGHEST, preferred_element_type=jnp.float32
        )
        - p_ref[...]
        + (mm(whi_, phi[...]) + mm(wlo_, phi[...]) + mm(whi_, plo[...]))
    )

    parts = a_send[0].astype(jnp.float32) * as_column(jnp.exp(tops[1] - lse), rows)
    for j in range(1, groups):
        arrived(PARTIAL, others[j], a_recv.at[others[j]])
        parts = parts + a_recv[others[j]].astype(jnp.float32) * as_column(jnp.exp(tops[j + 1] - lse), rows)
    qg_ref[...] = (qg_ref[...] + parts) * SCALE
    saves[1].start()
    sums = pg_ref[...]
    for s in range(1, 3):
        copies[GRAD, s].wait_recv()
        sums = sums + g_recv[s].astype(jnp.float32)
    pg_ref[...] = (sums - query) * SCALE
    saves[2].start()

    def loss_wait(k, carry):
        loss_copy(k).wait()
        return carry

    lax.fori_loop(1, loops, loss_wait, 0)
    loss_ref[0, 0] = jnp.sum(l_recv[:, 0:1, 0:1]) / (rows * loops * groups)
    for each in copies.values():
        each.wait_send()

    @pl.when(g < groups - 1)
    def _():
        own_right.wait_send()

    @pl.when(g > 0)
    def _():
        own_left.wait_send()

    for j in range(1, groups):
        valid, forward = onward(j)

        @pl.when(valid)
        def _():
            forward.wait_send()

    for save in saves:
        save.wait()


def hand_over(a_ref, b_ref, c_ref, a_out, b_out, c_out, a_here, b_here, c_here, sem_in, sem_out):
    trips = []
    for src, here, dst in ((c_ref, c_here, c_out), (a_ref, a_here, a_out), (b_ref, b_here, b_out)):
        part = src.shape[0] // 4
        for i in range(4):
            at, k = pl.ds(i * part, part), len(trips)
            trips.append((
                pltpu.make_async_copy(src.at[at], here.at[at], sem_in.at[k]),
                pltpu.make_async_copy(here.at[at], dst.at[at], sem_out.at[k]),
            ))
    for bring, _ in trips:
        bring.start()
    for bring, store in trips:
        bring.wait()
        store.start()
    for _, store in trips:
        store.wait()


def local(loops, groups, queries, passages, hard_table, hard_index):
    rows, width = queries.shape
    table_rows = hard_table.shape[0]
    index = hard_index.T
    anywhere = pl.BlockSpec(memory_space=pl.ANY)
    vmem = pl.BlockSpec(memory_space=pltpu.VMEM)
    f32, bf16, i16 = jnp.float32, jnp.bfloat16, jnp.int16
    out = pl.pallas_call(
        functools.partial(kernel, loops, groups),
        out_shape=(
            jax.ShapeDtypeStruct((1, 1), f32),
            jax.ShapeDtypeStruct((rows, width), f32),
            jax.ShapeDtypeStruct((rows, width), f32),
            jax.ShapeDtypeStruct((table_rows, width), bf16),
        ),
        in_specs=[anywhere] * 3 + [vmem],
        out_specs=(pl.BlockSpec(memory_space=pltpu.SMEM),) + (anywhere,) * 3,
        scratch_shapes=[
            pltpu.VMEM((rows, width), f32),
            pltpu.VMEM((rows, width), f32),
            pltpu.VMEM((table_rows, width), bf16),
            pltpu.VMEM((rows, width), f32),
            pltpu.VMEM((rows, width), f32),
            pltpu.VMEM((table_rows, width), bf16),
            pltpu.VMEM((groups, rows, width), i16),
            pltpu.VMEM((groups, 16, rows), f32),
            pltpu.VMEM((STOPS, rows, width), i16),
            pltpu.VMEM((STOPS, 8, rows), f32),
            pltpu.VMEM((groups, 8, rows), f32),
            pltpu.VMEM((groups, 8, rows), f32),
            pltpu.VMEM((groups, rows, width), bf16),
            pltpu.VMEM((groups, rows, width), bf16),
            pltpu.VMEM((8, rows), f32),
            pltpu.VMEM((groups, 8, rows), f32),
            pltpu.VMEM((STOPS, rows, width), bf16),
            pltpu.VMEM((STOPS, rows, width), bf16),
            pltpu.VMEM((8, rows), f32),
            pltpu.VMEM((loops, 8, rows), f32),
            pltpu.VMEM((groups, table_rows, rows), f32),
            pltpu.VMEM((groups, table_rows, rows), f32),
            pltpu.VMEM((STOPS * rows, rows), f32),
            pltpu.VMEM(((STOPS - 1) * rows, width), bf16),
            pltpu.VMEM(((STOPS - 1) * rows, width), bf16),
            pltpu.VMEM((STOPS - 1, rows, width), f32),
            pltpu.VMEM((groups * rows, width), bf16),
            pltpu.VMEM((groups * rows, width), bf16),
            pltpu.VMEM((table_rows, groups * rows), bf16),
            pltpu.SemaphoreType.DMA((8, max(groups, STOPS) + 1)),
            pltpu.SemaphoreType.DMA((8, max(groups, STOPS) + 1)),
            pltpu.SemaphoreType.DMA((loops,)),
            pltpu.SemaphoreType.DMA((loops,)),
            pltpu.SemaphoreType.DMA((3,)),
            pltpu.SemaphoreType.DMA((3,)),
        ],
        compiler_params=pltpu.CompilerParams(
            collective_id=0, has_side_effects=True, vmem_limit_bytes=60 * 1024 * 1024
        ),
    )(queries, passages, hard_table, index)
    done = pl.pallas_call(
        hand_over,
        out_shape=tuple(jax.ShapeDtypeStruct(x.shape, x.dtype) for x in out[1:]),
        in_specs=[anywhere] * 3,
        out_specs=(anywhere,) * 3,
        scratch_shapes=[pltpu.VMEM(x.shape, x.dtype) for x in out[1:]]
        + [pltpu.SemaphoreType.DMA((12,)), pltpu.SemaphoreType.DMA((12,))],
        compiler_params=pltpu.CompilerParams(vmem_limit_bytes=60 * 1024 * 1024),
    )(*out[1:])
    return (out[0].reshape(()),) + tuple(done)


def solution(mesh):
    rows = P(("blk", "grp"), None)
    return jax.shard_map(
        functools.partial(local, mesh.shape["blk"], mesh.shape["grp"]),
        mesh=mesh,
        in_specs=(rows, rows, rows, rows),
        out_specs=(P(), rows, rows, rows),
        check_vma=False,
    )
```

```python
import functools

import jax
import jax.numpy as jnp
from jax import lax
from jax.experimental import pallas as pl
from jax.experimental.pallas import tpu as pltpu
from jax.sharding import PartitionSpec as P

STOPS = 4
SCALE = 0.015625
TOP = 32766.0
LOW = -1e30
MESH = pl.DeviceIdType.MESH
HIGHEST = lax.Precision.HIGHEST

QUERY, QUERY_META, PASSAGE, PASSAGE_META, STATS, PARTIAL, LSE, GRAD, MERGE, MERGE_META = range(10)


def as_column(row, count):
    return jnp.broadcast_to(row, (128, count)).T[:, 0:1]


def as_row(column, count):
    return jnp.broadcast_to(column, (count, 128)).T[0:1, :]


def coded(value):
    largest = jnp.max(jnp.abs(value), axis=1, keepdims=True)
    largest = jnp.maximum(largest, 1e-30)
    code = jnp.round(value * (TOP / largest)).astype(jnp.int32).astype(jnp.int16)
    return code, largest * (1.0 / TOP)


def halves(code):
    value = code.astype(jnp.int32).astype(jnp.float32)
    high = value.astype(jnp.bfloat16)
    return high, (value - high.astype(jnp.float32)).astype(jnp.bfloat16)


def two_terms(value):
    high = value.astype(jnp.bfloat16)
    return high, (value - high.astype(jnp.float32)).astype(jnp.bfloat16)


def mm(a, b):
    return jnp.dot(a, b, preferred_element_type=jnp.float32)


def nt(a, b, precision=None):
    return lax.dot_general(
        a, b, (((1,), (1,)), ((), ())), precision=precision, preferred_element_type=jnp.float32
    )


def kernel(
    loops, groups,
    q_hbm, p_hbm, t_hbm, idx_ref,
    loss_ref, qg_out, pg_out, tg_out,
    q_ref, p_ref, t_ref, qg_ref, pg_ref, tg_ref, q16, qmeta, p16, pmeta, st_send, st_recv, a_send, a_recv, af, m_stat, m_recv, lse_send, lse_recv,
    g_send, g_recv, l_send, l_recv, sh, ch, sw, phi, plo, gf, qhi, qlo, whi,
    send_sem, recv_sem, lsend_sem, lrecv_sem, load_sem, save_sem,
):
    b = lax.axis_index("blk")
    g = lax.axis_index("grp")
    rows, width = q_ref.shape
    table_rows = t_ref.shape[0]
    loads = [
        pltpu.make_async_copy(src, dst, load_sem.at[i])
        for i, (src, dst) in enumerate(((q_hbm, q_ref), (p_hbm, p_ref), (t_hbm, t_ref)))
    ]
    for load in loads:
        load.start()
    barrier = pltpu.get_barrier_semaphore()
    for j in range(1, groups):
        pl.semaphore_signal(
            barrier, inc=1, device_id=(b, lax.rem(g + j, groups)), device_id_type=MESH
        )

    def greet(k, carry):
        pl.semaphore_signal(
            barrier, inc=1, device_id=(lax.rem(b + k, loops), g), device_id_type=MESH
        )
        return carry

    lax.fori_loop(1, loops, greet, 0)

    def copy(kind, j, src, dst, device, slot=None):
        return pltpu.make_async_remote_copy(
            src_ref=src,
            dst_ref=dst,
            send_sem=send_sem.at[kind, j],
            recv_sem=recv_sem.at[kind, j if slot is None else slot],
            device_id=device,
            device_id_type=MESH,
        )

    copies = {}

    def go(kind, j, src, dst, device, slot=None):
        copies[kind, j] = copy(kind, j, src, dst, device, slot)
        copies[kind, j].start()

    def arrived(kind, slot, ref):
        copy(kind, 0, ref, ref, (b, lax.rem(g + 1, groups)), slot).wait_recv()

    assert groups == 4
    half = g // 2
    inner = lax.rem(g, 2) == 1 - half
    near = inner.astype(jnp.int32)
    others = [None, g + 1 - 2 * lax.rem(g, 2), 2 - half, 3 - 3 * half]

    own_right = copy(QUERY, 0, q16.at[g], q16.at[g], (b, jnp.minimum(g + 1, groups - 1)), g)
    own_left = copy(QUERY, groups, q16.at[g], q16.at[g], (b, jnp.maximum(g - 1, 0)), g)

    def onward(j):
        src = others[j]
        step = jnp.where(src < g, 1, -1)
        dst = g + step
        return (dst >= 0) & (dst < groups), copy(
            QUERY, j, q16.at[src], q16.at[src], (b, jnp.clip(dst, 0, groups - 1)), src
        )

    def receive(j):
        src = others[j]
        arrived(QUERY, src, q16.at[src])
        valid, forward = onward(j)

        @pl.when(valid)
        def _():
            forward.start()

    loads[0].wait()
    query = q_ref[...]
    code, scale = coded(query)
    q16[g] = code
    qmeta[g, 0:8, :] = idx_ref[...].astype(jnp.float32)
    qmeta[g, 8:16, :] = jnp.broadcast_to(as_row(scale, rows), (8, rows))
    pl.semaphore_wait(barrier, groups - 1 + loops - 1)

    @pl.when(g < groups - 1)
    def _():
        own_right.start()

    @pl.when(g > 0)
    def _():
        own_left.start()

    for j in range(1, groups):
        go(QUERY_META, j, qmeta.at[g], qmeta.at[g], (b, others[j]), g)
    loads[1].wait()
    code, scale = coded(p_ref[...])
    p16[0] = code
    pmeta[0] = jnp.broadcast_to(as_row(scale, rows), (8, rows))
    for s in range(1, STOPS):
        go(PASSAGE_META, s, pmeta.at[0], pmeta.at[s], (lax.rem(b + s, loops), g))
    for s in (3, 1):
        go(PASSAGE, s, p16.at[0], p16.at[s], (lax.rem(b + s, loops), g))
    loads[2].wait()

    row_id = lax.broadcasted_iota(jnp.int32, (table_rows, rows), 0).astype(jnp.float32) + (
        g * table_rows
    ).astype(jnp.float32)

    def count(j):
        src = g if j == 0 else others[j]
        named = jnp.zeros((table_rows, rows), jnp.float32)
        for k in range(8):
            named = named + jnp.where(row_id == qmeta[src, k:k + 1, :], 1.0, 0.0)
        ch[j] = named

    def hard_part(j):
        src = g if j == 0 else others[j]
        high, low = halves(q16[src])
        qhi[j * rows:(j + 1) * rows, :] = high
        qlo[j * rows:(j + 1) * rows, :] = low
        table = t_ref[...]
        both = nt(table, jnp.concatenate([high, low], axis=0))
        scores = (both[:, 0:rows] + both[:, rows:]) * (qmeta[src, 8:9, :] * SCALE)
        named = ch[j]
        top = jnp.max(jnp.where(named > 0.0, scores, LOW), axis=0, keepdims=True)
        part = named * jnp.exp(jnp.minimum(scores - top, 0.0))
        sh[j] = scores
        st_send[j, 0:1, :] = top
        st_send[j, 1:2, :] = jnp.sum(part, axis=0, keepdims=True)
        if j > 0:
            go(STATS, j, st_send.at[j], st_recv.at[g], (b, src), g)
        partial = mm(part.T.astype(jnp.bfloat16), table)
        if j == 0:
            af[0] = partial
        elif j == 1:
            a_send[j] = partial.astype(jnp.bfloat16)
            go(PARTIAL, j, a_send.at[j], a_recv.at[0], (b, src), 0)
        else:
            af[j - 1] = partial

            @pl.when(jnp.logical_not(inner))
            def _():
                a_send[j] = partial.astype(jnp.bfloat16)
                merge_stats(j).start()
                merge_block(j).start()

    def merge_stats(j):
        return copy(MERGE_META, j, st_send.at[j], m_stat.at[j - 2], (b, others[1]))

    def merge_block(j):
        return copy(MERGE, j, a_send.at[j], m_recv.at[j - 2], (b, others[1]))

    def joined_block(j):
        return copy(PARTIAL, j, a_send.at[j], a_recv.at[1], (b, others[j]), 1)

    def join(j):
        @pl.when(inner)
        def _():
            merge_stats(j).wait_recv()
            merge_block(j).wait_recv()
            here, there = st_send[j, 0:1, :], m_stat[j - 2, 0:1, :]
            most = jnp.maximum(here, there)
            a_send[j] = (
                af[j - 1] * as_column(jnp.exp(here - most), rows)
                + m_recv[j - 2].astype(jnp.float32) * as_column(jnp.exp(there - most), rows)
            ).astype(jnp.bfloat16)
            joined_block(j).start()

    def window_part(s):
        if s == 0:
            sw[0:rows, :] = nt(p_ref[...], query, HIGHEST) * SCALE
            return
        high, low = halves(p16[s])
        at = slice((s - 1) * rows, s * rows)
        phi[at, :] = high
        plo[at, :] = low
        own_high, own_low = qhi[0:rows, :], qlo[0:rows, :]
        both = nt(high, jnp.concatenate([own_high, own_low], axis=0))
        scores = both[:, 0:rows] + both[:, rows:] + nt(low, own_high)
        sw[s * rows:(s + 1) * rows, :] = (
            scores * as_column(pmeta[s, 0:1, :], rows) * (qmeta[g, 8:9, :] * SCALE)
        )

    st_send[...] = jnp.zeros_like(st_send)
    count(0)
    hard_part(0)
    window_part(0)
    for j in range(1, groups):
        arrived(QUERY_META, others[j], qmeta.at[others[j]])
        count(j)
    positive = jnp.sum(query * p_ref[...]) * SCALE
    def window_next(s):
        copies[PASSAGE_META, s].wait_recv()
        if s == 2:
            copies[PASSAGE, s].wait_recv()
        window_part(s)

    receive(1)
    if groups > 2:

        @pl.when(near > 0)
        def _():
            receive(2)

    hard_part(1)
    if groups > 2:

        @pl.when(near == 0)
        def _():
            receive(2)

    odd = lax.rem(b, 2)
    partner = b + 1 - 2 * odd
    for s in (1, 3):
        copies[PASSAGE, s].wait_recv()
    go(PASSAGE, 2, p16.at[1 + 2 * odd], p16.at[2], (partner, g))
    window_next(1)

    @pl.when(near > 0)
    def _():
        receive(3)

    hard_part(2)

    @pl.when(near == 0)
    def _():
        receive(3)

    for s in range(2, STOPS):
        window_next(s)
    hard_part(3)
    join(2)

    window = sw[...]
    tops = [jnp.max(window, axis=0, keepdims=True), st_send[0, 0:1, :]]
    for j in range(1, groups):
        arrived(STATS, others[j], st_recv.at[others[j]])
        tops.append(st_recv[others[j], 0:1, :])
    top = functools.reduce(jnp.maximum, tops)
    total = jnp.sum(jnp.exp(window - top), axis=0, keepdims=True)
    total = total + st_send[0, 1:2, :] * jnp.exp(tops[1] - top)
    for j in range(1, groups):
        total = total + st_recv[others[j], 1:2, :] * jnp.exp(tops[j + 1] - top)
    lse = top + jnp.log(total)
    lse_send[0:1, :] = lse
    lse_send[1:8, :] = jnp.broadcast_to(jnp.sum(lse) - positive, (7, rows))
    for j in range(1, groups):
        go(LSE, j, lse_send, lse_recv.at[g], (b, others[j]), g)

    sw[...] = jnp.exp(window - lse)
    whi_, wlo_ = two_terms(sw[rows:, :] * qmeta[g, 8:9, :])
    terms = mm(
        jnp.concatenate([whi_, whi_], axis=1),
        jnp.concatenate([qhi[0:rows, :], qlo[0:rows, :]], axis=0),
    ) + mm(wlo_, qhi[0:rows, :])
    alone, joined = 3 - 2 * odd, 1 + 2 * odd
    for s in range(1, STOPS):
        term = terms[(s - 1) * rows:s * rows, :]
        gf[s - 1] = term
        g_send[s - 1] = term.astype(jnp.bfloat16)
    go(GRAD, 0, g_send.at[1], g_recv.at[0], (partner, g))
    go(GRAD, 1, g_send.at[alone - 1], g_recv.at[1], (lax.rem(b + loops - alone, loops), g))
    pg_ref[...] = jnp.dot(
        sw[0:rows, :], query, precision=HIGHEST, preferred_element_type=jnp.float32
    )

    join(3)
    group_loss = lse_send[1:2, :]
    whi[:, 0:rows] = (
        ch[0] * jnp.exp(jnp.minimum(sh[0] - lse, 0.0)) * (qmeta[g, 8:9, :] * SCALE)
    ).astype(jnp.bfloat16)
    for j in range(1, groups):
        arrived(LSE, others[j], lse_recv.at[others[j]])
        group_loss = group_loss + lse_recv[others[j], 1:2, :]
        whi[:, j * rows:(j + 1) * rows] = jnp.where(
            ch[j] > 0.0,
            ch[j] * jnp.exp(jnp.minimum(sh[j] - lse_recv[others[j], 0:1, :], 0.0)) * (qmeta[others[j], 8:9, :] * SCALE),
            0.0,
        ).astype(jnp.bfloat16)

    l_send[...] = jnp.broadcast_to(group_loss, (8, rows))
    l_recv[0] = jnp.broadcast_to(group_loss, (8, rows))

    def loss_copy(k):
        return pltpu.make_async_remote_copy(
            src_ref=l_send,
            dst_ref=l_recv.at[k],
            send_sem=lsend_sem.at[k],
            recv_sem=lrecv_sem.at[k],
            device_id=(lax.rem(b + k, loops), g),
            device_id_type=MESH,
        )

    def loss_start(k, carry):
        loss_copy(k).start()
        return carry

    lax.fori_loop(1, loops, loss_start, 0)

    copies[GRAD, 0].wait_recv()
    g_send[STOPS - 1] = (gf[joined - 1] + g_recv[0].astype(jnp.float32)).astype(jnp.bfloat16)
    go(GRAD, 2, g_send.at[STOPS - 1], g_recv.at[2], (lax.rem(b + loops - joined, loops), g))

    tile = 256

    def table_tile(step, carry):
        cols = pl.ds(pl.multiple_of(step * tile, tile), tile)
        left = whi[...]
        tg_ref[:, cols] = (
            jnp.dot(left, qhi[:, cols], preferred_element_type=jnp.float32)
            + jnp.dot(left, qlo[:, cols], preferred_element_type=jnp.float32)
        ).astype(jnp.bfloat16)
        return carry

    lax.fori_loop(0, width // tile, table_tile, 0)
    saves = [
        pltpu.make_async_copy(src, dst, save_sem.at[i])
        for i, (src, dst) in enumerate(((tg_ref, tg_out), (qg_ref, qg_out), (pg_ref, pg_out)))
    ]
    saves[0].start()

    whi_, wlo_ = two_terms(
        jnp.concatenate(
            [
                sw[s * rows:(s + 1) * rows, :] * as_column(pmeta[s, 0:1, :], rows)
                for s in range(1, STOPS)
            ],
            axis=0,
        ).T
    )
    qg_ref[...] = (
        jnp.dot(
            sw[0:rows, :].T, p_ref[...], precision=HIGHEST, preferred_element_type=jnp.float32
        )
        - p_ref[...]
        + (mm(whi_, phi[...]) + mm(wlo_, phi[...]) + mm(whi_, plo[...]))
    )

    arrived(PARTIAL, 0, a_recv.at[0])
    arrived(PARTIAL, 1, a_recv.at[1])
    parts = (
        af[0] * as_column(jnp.exp(tops[1] - lse), rows)
        + a_recv[0].astype(jnp.float32) * as_column(jnp.exp(tops[2] - lse), rows)
        + a_recv[1].astype(jnp.float32)
        * as_column(jnp.exp(jnp.maximum(tops[3], tops[4]) - lse), rows)
    )
    qg_ref[...] = (qg_ref[...] + parts) * SCALE
    saves[1].start()
    sums = pg_ref[...]
    for s in range(1, 3):
        copies[GRAD, s].wait_recv()
        sums = sums + g_recv[s].astype(jnp.float32)
    pg_ref[...] = (sums - query) * SCALE
    saves[2].start()

    def loss_wait(k, carry):
        loss_copy(k).wait()
        return carry

    lax.fori_loop(1, loops, loss_wait, 0)
    loss_ref[0, 0] = jnp.sum(l_recv[:, 0:1, 0:1]) / (rows * loops * groups)
    for each in copies.values():
        each.wait_send()

    for j in range(2, groups):

        @pl.when(inner)
        def _():
            joined_block(j).wait_send()

        @pl.when(jnp.logical_not(inner))
        def _():
            merge_stats(j).wait_send()
            merge_block(j).wait_send()

    @pl.when(g < groups - 1)
    def _():
        own_right.wait_send()

    @pl.when(g > 0)
    def _():
        own_left.wait_send()

    for j in range(1, groups):
        valid, forward = onward(j)

        @pl.when(valid)
        def _():
            forward.wait_send()

    for save in saves:
        save.wait()


def hand_over(a_ref, b_ref, c_ref, a_out, b_out, c_out, a_here, b_here, c_here, sem_in, sem_out):
    trips = []
    for src, here, dst in ((c_ref, c_here, c_out), (a_ref, a_here, a_out), (b_ref, b_here, b_out)):
        part = src.shape[0] // 4
        for i in range(4):
            at, k = pl.ds(i * part, part), len(trips)
            trips.append((
                pltpu.make_async_copy(src.at[at], here.at[at], sem_in.at[k]),
                pltpu.make_async_copy(here.at[at], dst.at[at], sem_out.at[k]),
            ))
    for bring, _ in trips:
        bring.start()
    for bring, store in trips:
        bring.wait()
        store.start()
    for _, store in trips:
        store.wait()


def local(loops, groups, queries, passages, hard_table, hard_index):
    rows, width = queries.shape
    table_rows = hard_table.shape[0]
    index = hard_index.T
    anywhere = pl.BlockSpec(memory_space=pl.ANY)
    vmem = pl.BlockSpec(memory_space=pltpu.VMEM)
    f32, bf16, i16 = jnp.float32, jnp.bfloat16, jnp.int16
    out = pl.pallas_call(
        functools.partial(kernel, loops, groups),
        out_shape=(
            jax.ShapeDtypeStruct((1, 1), f32),
            jax.ShapeDtypeStruct((rows, width), f32),
            jax.ShapeDtypeStruct((rows, width), f32),
            jax.ShapeDtypeStruct((table_rows, width), bf16),
        ),
        in_specs=[anywhere] * 3 + [vmem],
        out_specs=(pl.BlockSpec(memory_space=pltpu.SMEM),) + (anywhere,) * 3,
        scratch_shapes=[
            pltpu.VMEM((rows, width), f32),
            pltpu.VMEM((rows, width), f32),
            pltpu.VMEM((table_rows, width), bf16),
            pltpu.VMEM((rows, width), f32),
            pltpu.VMEM((rows, width), f32),
            pltpu.VMEM((table_rows, width), bf16),
            pltpu.VMEM((groups, rows, width), i16),
            pltpu.VMEM((groups, 16, rows), f32),
            pltpu.VMEM((STOPS, rows, width), i16),
            pltpu.VMEM((STOPS, 8, rows), f32),
            pltpu.VMEM((groups, 8, rows), f32),
            pltpu.VMEM((groups, 8, rows), f32),
            pltpu.VMEM((groups, rows, width), bf16),
            pltpu.VMEM((2, rows, width), bf16),
            pltpu.VMEM((groups - 1, rows, width), f32),
            pltpu.VMEM((2, 8, rows), f32),
            pltpu.VMEM((2, rows, width), bf16),
            pltpu.VMEM((8, rows), f32),
            pltpu.VMEM((groups, 8, rows), f32),
            pltpu.VMEM((STOPS, rows, width), bf16),
            pltpu.VMEM((STOPS, rows, width), bf16),
            pltpu.VMEM((8, rows), f32),
            pltpu.VMEM((loops, 8, rows), f32),
            pltpu.VMEM((groups, table_rows, rows), f32),
            pltpu.VMEM((groups, table_rows, rows), f32),
            pltpu.VMEM((STOPS * rows, rows), f32),
            pltpu.VMEM(((STOPS - 1) * rows, width), bf16),
            pltpu.VMEM(((STOPS - 1) * rows, width), bf16),
            pltpu.VMEM((STOPS - 1, rows, width), f32),
            pltpu.VMEM((groups * rows, width), bf16),
            pltpu.VMEM((groups * rows, width), bf16),
            pltpu.VMEM((table_rows, groups * rows), bf16),
            pltpu.SemaphoreType.DMA((10, max(groups, STOPS) + 1)),
            pltpu.SemaphoreType.DMA((10, max(groups, STOPS) + 1)),
            pltpu.SemaphoreType.DMA((loops,)),
            pltpu.SemaphoreType.DMA((loops,)),
            pltpu.SemaphoreType.DMA((3,)),
            pltpu.SemaphoreType.DMA((3,)),
        ],
        compiler_params=pltpu.CompilerParams(
            collective_id=0, has_side_effects=True, vmem_limit_bytes=60 * 1024 * 1024
        ),
    )(queries, passages, hard_table, index)
    done = pl.pallas_call(
        hand_over,
        out_shape=tuple(jax.ShapeDtypeStruct(x.shape, x.dtype) for x in out[1:]),
        in_specs=[anywhere] * 3,
        out_specs=(anywhere,) * 3,
        scratch_shapes=[pltpu.VMEM(x.shape, x.dtype) for x in out[1:]]
        + [pltpu.SemaphoreType.DMA((12,)), pltpu.SemaphoreType.DMA((12,))],
        compiler_params=pltpu.CompilerParams(vmem_limit_bytes=60 * 1024 * 1024),
    )(*out[1:])
    return (out[0].reshape(()),) + tuple(done)


def solution(mesh):
    rows = P(("blk", "grp"), None)
    return jax.shard_map(
        functools.partial(local, mesh.shape["blk"], mesh.shape["grp"]),
        mesh=mesh,
        in_specs=(rows, rows, rows, rows),
        out_specs=(P(), rows, rows, rows),
        check_vma=False,
    )
```

```python
import functools

import jax
import jax.numpy as jnp
from jax import lax
from jax.experimental import pallas as pl
from jax.experimental.pallas import tpu as pltpu
from jax.sharding import PartitionSpec as P

STOPS = 4
SCALE = 0.015625
TOP = 32766.0
LOW = -1e30
MESH = pl.DeviceIdType.MESH
HIGHEST = lax.Precision.HIGHEST

QUERY, QUERY_META, PASSAGE, PASSAGE_META, STATS, PARTIAL, LSE, GRAD, MERGE, MERGE_META = range(10)


def as_column(row, count):
    return jnp.broadcast_to(row, (128, count)).T[:, 0:1]


def as_row(column, count):
    return jnp.broadcast_to(column, (count, 128)).T[0:1, :]


def coded(value):
    largest = jnp.max(jnp.abs(value), axis=1, keepdims=True)
    largest = jnp.maximum(largest, 1e-30)
    code = jnp.round(value * (TOP / largest)).astype(jnp.int32).astype(jnp.int16)
    return code, largest * (1.0 / TOP)


def halves(code):
    value = code.astype(jnp.int32).astype(jnp.float32)
    high = value.astype(jnp.bfloat16)
    return high, (value - high.astype(jnp.float32)).astype(jnp.bfloat16)


def two_terms(value):
    high = value.astype(jnp.bfloat16)
    return high, (value - high.astype(jnp.float32)).astype(jnp.bfloat16)


def mm(a, b):
    return jnp.dot(a, b, preferred_element_type=jnp.float32)


def nt(a, b, precision=None):
    return lax.dot_general(
        a, b, (((1,), (1,)), ((), ())), precision=precision, preferred_element_type=jnp.float32
    )


def kernel(
    loops, groups,
    q_hbm, p_hbm, t_hbm, idx_ref,
    loss_ref, qg_out, pg_out, tg_out,
    q_ref, p_ref, t_ref, qg_ref, pg_ref, tg_ref, q16, qmeta, p16, pmeta, st_send, st_recv, a_send, a_recv, af, m_stat, m_recv, lse_send, lse_recv,
    g_send, g_recv, l_send, l_recv, ch, sw, phi, plo, gf, qhi, qlo, whi, w_top,
    send_sem, recv_sem, lsend_sem, lrecv_sem, load_sem, save_sem,
):
    b = lax.axis_index("blk")
    g = lax.axis_index("grp")
    rows, width = q_ref.shape
    table_rows = t_ref.shape[0]
    loads = [
        pltpu.make_async_copy(src, dst, load_sem.at[i])
        for i, (src, dst) in enumerate(((q_hbm, q_ref), (p_hbm, p_ref), (t_hbm, t_ref)))
    ]
    for load in loads:
        load.start()
    barrier = pltpu.get_barrier_semaphore()
    for j in range(1, groups):
        pl.semaphore_signal(
            barrier, inc=1, device_id=(b, lax.rem(g + j, groups)), device_id_type=MESH
        )

    def greet(k, carry):
        pl.semaphore_signal(
            barrier, inc=1, device_id=(lax.rem(b + k, loops), g), device_id_type=MESH
        )
        return carry

    lax.fori_loop(1, loops, greet, 0)

    def copy(kind, j, src, dst, device, slot=None):
        return pltpu.make_async_remote_copy(
            src_ref=src,
            dst_ref=dst,
            send_sem=send_sem.at[kind, j],
            recv_sem=recv_sem.at[kind, j if slot is None else slot],
            device_id=device,
            device_id_type=MESH,
        )

    copies = {}

    def go(kind, j, src, dst, device, slot=None):
        copies[kind, j] = copy(kind, j, src, dst, device, slot)
        copies[kind, j].start()

    def arrived(kind, slot, ref):
        copy(kind, 0, ref, ref, (b, lax.rem(g + 1, groups)), slot).wait_recv()

    assert groups == 4
    half = g // 2
    inner = lax.rem(g, 2) == 1 - half
    near = inner.astype(jnp.int32)
    others = [None, g + 1 - 2 * lax.rem(g, 2), 2 - half, 3 - 3 * half]

    own_right = copy(QUERY, 0, q16.at[g], q16.at[g], (b, jnp.minimum(g + 1, groups - 1)), g)
    own_left = copy(QUERY, groups, q16.at[g], q16.at[g], (b, jnp.maximum(g - 1, 0)), g)

    def onward(j):
        src = others[j]
        step = jnp.where(src < g, 1, -1)
        dst = g + step
        return (dst >= 0) & (dst < groups), copy(
            QUERY, j, q16.at[src], q16.at[src], (b, jnp.clip(dst, 0, groups - 1)), src
        )

    def receive(j):
        src = others[j]
        arrived(QUERY, src, q16.at[src])
        valid, forward = onward(j)

        @pl.when(valid)
        def _():
            forward.start()

    loads[0].wait()
    query = q_ref[...]
    code, scale = coded(query)
    q16[g] = code
    qmeta[g, 0:8, :] = idx_ref[...].astype(jnp.float32)
    qmeta[g, 8:16, :] = jnp.broadcast_to(as_row(scale, rows), (8, rows))
    pl.semaphore_wait(barrier, groups - 1 + loops - 1)

    @pl.when(g < groups - 1)
    def _():
        own_right.start()

    @pl.when(g > 0)
    def _():
        own_left.start()

    for j in range(1, groups):
        go(QUERY_META, j, qmeta.at[g], qmeta.at[g], (b, others[j]), g)
    loads[1].wait()
    code, scale = coded(p_ref[...])
    p16[0] = code
    pmeta[0] = jnp.broadcast_to(as_row(scale, rows), (8, rows))
    for s in range(1, STOPS):
        go(PASSAGE_META, s, pmeta.at[0], pmeta.at[s], (lax.rem(b + s, loops), g))
    for s in (3, 1):
        go(PASSAGE, s, p16.at[0], p16.at[s], (lax.rem(b + s, loops), g))
    loads[2].wait()

    row_id = lax.broadcasted_iota(jnp.int32, (table_rows, rows), 0).astype(jnp.float32) + (
        g * table_rows
    ).astype(jnp.float32)

    def count(j):
        src = g if j == 0 else others[j]
        named = jnp.zeros((table_rows, rows), jnp.float32)
        for k in range(8):
            named = named + jnp.where(row_id == qmeta[src, k:k + 1, :], 1.0, 0.0)
        ch[j] = named

    def hard_part(j):
        src = g if j == 0 else others[j]
        high, low = halves(q16[src])
        qhi[j * rows:(j + 1) * rows, :] = high
        qlo[j * rows:(j + 1) * rows, :] = low
        table = t_ref[...]
        both = nt(table, jnp.concatenate([high, low], axis=0))
        scores = (both[:, 0:rows] + both[:, rows:]) * (qmeta[src, 8:9, :] * SCALE)
        named = ch[j]
        top = jnp.max(jnp.where(named > 0.0, scores, LOW), axis=0, keepdims=True)
        part = named * jnp.exp(jnp.minimum(scores - top, 0.0))
        ch[j] = part
        st_send[j, 0:1, :] = top
        st_send[j, 1:2, :] = jnp.sum(part, axis=0, keepdims=True)
        if j > 0:
            go(STATS, j, st_send.at[j], st_recv.at[g], (b, src), g)
        partial = mm(part.T.astype(jnp.bfloat16), table)
        if j == 0:
            af[0] = partial
        elif j == 1:
            a_send[j] = partial.astype(jnp.bfloat16)
            go(PARTIAL, j, a_send.at[j], a_recv.at[0], (b, src), 0)
        else:
            af[j - 1] = partial

            @pl.when(jnp.logical_not(inner))
            def _():
                a_send[j] = partial.astype(jnp.bfloat16)
                merge_stats(j).start()
                merge_block(j).start()

    def merge_stats(j):
        return copy(MERGE_META, j, st_send.at[j], m_stat.at[j - 2], (b, others[1]))

    def merge_block(j):
        return copy(MERGE, j, a_send.at[j], m_recv.at[j - 2], (b, others[1]))

    def joined_block(j):
        return copy(PARTIAL, j, a_send.at[j], a_recv.at[1], (b, others[j]), 1)

    def join(j):
        @pl.when(inner)
        def _():
            merge_stats(j).wait_recv()
            merge_block(j).wait_recv()
            here, there = st_send[j, 0:1, :], m_stat[j - 2, 0:1, :]
            most = jnp.maximum(here, there)
            a_send[j] = (
                af[j - 1] * as_column(jnp.exp(here - most), rows)
                + m_recv[j - 2].astype(jnp.float32) * as_column(jnp.exp(there - most), rows)
            ).astype(jnp.bfloat16)
            joined_block(j).start()

    def window_part(s):
        if s == 0:
            sw[0:rows, :] = nt(p_ref[...], query, HIGHEST) * SCALE
            return
        high, low = halves(p16[s])
        at = slice((s - 1) * rows, s * rows)
        phi[at, :] = high
        plo[at, :] = low
        own_high, own_low = qhi[0:rows, :], qlo[0:rows, :]
        both = nt(high, jnp.concatenate([own_high, own_low], axis=0))
        scores = both[:, 0:rows] + both[:, rows:] + nt(low, own_high)
        sw[s * rows:(s + 1) * rows, :] = (
            scores * as_column(pmeta[s, 0:1, :], rows) * (qmeta[g, 8:9, :] * SCALE)
        )

    def window_grad():
        top = jnp.max(sw[...], axis=0, keepdims=True)
        sw[...] = jnp.exp(sw[...] - top)
        w_top[...] = jnp.broadcast_to(top, (8, rows))
        high, low = two_terms(
            jnp.concatenate(
                [
                    sw[s * rows:(s + 1) * rows, :] * as_column(pmeta[s, 0:1, :], rows)
                    for s in range(1, STOPS)
                ],
                axis=0,
            ).T
        )
        qg_ref[...] = jnp.dot(
            sw[0:rows, :].T, p_ref[...], precision=HIGHEST, preferred_element_type=jnp.float32
        ) + (mm(high, phi[...]) + mm(low, phi[...]) + mm(high, plo[...]))

    st_send[...] = jnp.zeros_like(st_send)
    count(0)
    hard_part(0)
    window_part(0)
    for j in range(1, groups):
        arrived(QUERY_META, others[j], qmeta.at[others[j]])
        count(j)
    positive = jnp.sum(query * p_ref[...]) * SCALE
    def window_next(s):
        copies[PASSAGE_META, s].wait_recv()
        if s == 2:
            copies[PASSAGE, s].wait_recv()
        window_part(s)

    receive(1)
    if groups > 2:

        @pl.when(near > 0)
        def _():
            receive(2)

    hard_part(1)
    if groups > 2:

        @pl.when(near == 0)
        def _():
            receive(2)

    odd = lax.rem(b, 2)
    partner = b + 1 - 2 * odd
    for s in (1, 3):
        copies[PASSAGE, s].wait_recv()
    go(PASSAGE, 2, p16.at[1 + 2 * odd], p16.at[2], (partner, g))
    window_next(1)

    @pl.when(near > 0)
    def _():
        receive(3)

    hard_part(2)

    for s in range(2, STOPS):
        window_next(s)

    @pl.when(near == 0)
    def _():
        window_grad()
        receive(3)

    hard_part(3)

    @pl.when(near > 0)
    def _():
        window_grad()

    join(2)

    tops = [w_top[0:1, :], st_send[0, 0:1, :]]
    for j in range(1, groups):
        arrived(STATS, others[j], st_recv.at[others[j]])
        tops.append(st_recv[others[j], 0:1, :])
    top = functools.reduce(jnp.maximum, tops)
    total = jnp.sum(sw[...], axis=0, keepdims=True) * jnp.exp(tops[0] - top)
    total = total + st_send[0, 1:2, :] * jnp.exp(tops[1] - top)
    for j in range(1, groups):
        total = total + st_recv[others[j], 1:2, :] * jnp.exp(tops[j + 1] - top)
    lse = top + jnp.log(total)
    lse_send[0:1, :] = lse
    lse_send[1:8, :] = jnp.broadcast_to(jnp.sum(lse) - positive, (7, rows))
    for j in range(1, groups):
        go(LSE, j, lse_send, lse_recv.at[g], (b, others[j]), g)

    sw[...] = sw[...] * jnp.exp(tops[0] - lse)
    whi_, wlo_ = two_terms(sw[rows:, :] * qmeta[g, 8:9, :])
    terms = mm(
        jnp.concatenate([whi_, whi_], axis=1),
        jnp.concatenate([qhi[0:rows, :], qlo[0:rows, :]], axis=0),
    ) + mm(wlo_, qhi[0:rows, :])
    alone, joined = 3 - 2 * odd, 1 + 2 * odd
    for s in range(1, STOPS):
        term = terms[(s - 1) * rows:s * rows, :]
        gf[s - 1] = term
        g_send[s - 1] = term.astype(jnp.bfloat16)
    go(GRAD, 0, g_send.at[1], g_recv.at[0], (partner, g))
    go(GRAD, 1, g_send.at[alone - 1], g_recv.at[1], (lax.rem(b + loops - alone, loops), g))
    pg_ref[...] = jnp.dot(
        sw[0:rows, :], query, precision=HIGHEST, preferred_element_type=jnp.float32
    )

    copies[GRAD, 0].wait_recv()
    g_send[STOPS - 1] = (gf[joined - 1] + g_recv[0].astype(jnp.float32)).astype(jnp.bfloat16)
    go(GRAD, 2, g_send.at[STOPS - 1], g_recv.at[2], (lax.rem(b + loops - joined, loops), g))
    join(3)
    group_loss = lse_send[1:2, :]
    whi[:, 0:rows] = (
        ch[0] * (jnp.exp(tops[1] - lse) * (qmeta[g, 8:9, :] * SCALE))
    ).astype(jnp.bfloat16)
    for j in range(1, groups):
        src = others[j]
        arrived(LSE, src, lse_recv.at[src])
        group_loss = group_loss + lse_recv[src, 1:2, :]
        factor = jnp.exp(jnp.minimum(st_send[j, 0:1, :] - lse_recv[src, 0:1, :], 0.0))
        whi[:, j * rows:(j + 1) * rows] = (
            ch[j] * (factor * (qmeta[src, 8:9, :] * SCALE))
        ).astype(jnp.bfloat16)

    l_send[...] = jnp.broadcast_to(group_loss, (8, rows))
    l_recv[0] = jnp.broadcast_to(group_loss, (8, rows))

    def loss_copy(k):
        return pltpu.make_async_remote_copy(
            src_ref=l_send,
            dst_ref=l_recv.at[k],
            send_sem=lsend_sem.at[k],
            recv_sem=lrecv_sem.at[k],
            device_id=(lax.rem(b + k, loops), g),
            device_id_type=MESH,
        )

    def loss_start(k, carry):
        loss_copy(k).start()
        return carry

    lax.fori_loop(1, loops, loss_start, 0)

    tile = 256

    def table_tile(step, carry):
        cols = pl.ds(pl.multiple_of(step * tile, tile), tile)
        left = whi[...]
        tg_ref[:, cols] = (
            jnp.dot(left, qhi[:, cols], preferred_element_type=jnp.float32)
            + jnp.dot(left, qlo[:, cols], preferred_element_type=jnp.float32)
        ).astype(jnp.bfloat16)
        return carry

    lax.fori_loop(0, width // tile, table_tile, 0)
    saves = [
        pltpu.make_async_copy(src, dst, save_sem.at[i])
        for i, (src, dst) in enumerate(((tg_ref, tg_out), (qg_ref, qg_out), (pg_ref, pg_out)))
    ]
    saves[0].start()

    qg_ref[...] = (
        qg_ref[...] * as_column(jnp.exp(tops[0] - lse), rows)
        + af[0] * as_column(jnp.exp(tops[1] - lse), rows)
        - p_ref[...]
    )
    arrived(PARTIAL, 0, a_recv.at[0])
    parts = a_recv[0].astype(jnp.float32) * as_column(jnp.exp(tops[2] - lse), rows)
    arrived(PARTIAL, 1, a_recv.at[1])
    parts = parts + a_recv[1].astype(jnp.float32) * as_column(
        jnp.exp(jnp.maximum(tops[3], tops[4]) - lse), rows
    )
    qg_ref[...] = (qg_ref[...] + parts) * SCALE
    saves[1].start()
    sums = pg_ref[...]
    for s in range(1, 3):
        copies[GRAD, s].wait_recv()
        sums = sums + g_recv[s].astype(jnp.float32)
    pg_ref[...] = (sums - query) * SCALE
    saves[2].start()

    def loss_wait(k, carry):
        loss_copy(k).wait()
        return carry

    lax.fori_loop(1, loops, loss_wait, 0)
    loss_ref[0, 0] = jnp.sum(l_recv[:, 0:1, 0:1]) / (rows * loops * groups)
    for each in copies.values():
        each.wait_send()

    for j in range(2, groups):

        @pl.when(inner)
        def _():
            joined_block(j).wait_send()

        @pl.when(jnp.logical_not(inner))
        def _():
            merge_stats(j).wait_send()
            merge_block(j).wait_send()

    @pl.when(g < groups - 1)
    def _():
        own_right.wait_send()

    @pl.when(g > 0)
    def _():
        own_left.wait_send()

    for j in range(1, groups):
        valid, forward = onward(j)

        @pl.when(valid)
        def _():
            forward.wait_send()

    for save in saves:
        save.wait()


def hand_over(a_ref, b_ref, c_ref, a_out, b_out, c_out, a_here, b_here, c_here, sem_in, sem_out):
    trips = []
    for src, here, dst in ((c_ref, c_here, c_out), (a_ref, a_here, a_out), (b_ref, b_here, b_out)):
        part = src.shape[0] // 4
        for i in range(4):
            at, k = pl.ds(i * part, part), len(trips)
            trips.append((
                pltpu.make_async_copy(src.at[at], here.at[at], sem_in.at[k]),
                pltpu.make_async_copy(here.at[at], dst.at[at], sem_out.at[k]),
            ))
    for bring, _ in trips:
        bring.start()
    for bring, store in trips:
        bring.wait()
        store.start()
    for _, store in trips:
        store.wait()


def local(loops, groups, queries, passages, hard_table, hard_index):
    rows, width = queries.shape
    table_rows = hard_table.shape[0]
    index = hard_index.T
    anywhere = pl.BlockSpec(memory_space=pl.ANY)
    vmem = pl.BlockSpec(memory_space=pltpu.VMEM)
    f32, bf16, i16 = jnp.float32, jnp.bfloat16, jnp.int16
    out = pl.pallas_call(
        functools.partial(kernel, loops, groups),
        out_shape=(
            jax.ShapeDtypeStruct((1, 1), f32),
            jax.ShapeDtypeStruct((rows, width), f32),
            jax.ShapeDtypeStruct((rows, width), f32),
            jax.ShapeDtypeStruct((table_rows, width), bf16),
        ),
        in_specs=[anywhere] * 3 + [vmem],
        out_specs=(pl.BlockSpec(memory_space=pltpu.SMEM),) + (anywhere,) * 3,
        scratch_shapes=[
            pltpu.VMEM((rows, width), f32),
            pltpu.VMEM((rows, width), f32),
            pltpu.VMEM((table_rows, width), bf16),
            pltpu.VMEM((rows, width), f32),
            pltpu.VMEM((rows, width), f32),
            pltpu.VMEM((table_rows, width), bf16),
            pltpu.VMEM((groups, rows, width), i16),
            pltpu.VMEM((groups, 16, rows), f32),
            pltpu.VMEM((STOPS, rows, width), i16),
            pltpu.VMEM((STOPS, 8, rows), f32),
            pltpu.VMEM((groups, 8, rows), f32),
            pltpu.VMEM((groups, 8, rows), f32),
            pltpu.VMEM((groups, rows, width), bf16),
            pltpu.VMEM((2, rows, width), bf16),
            pltpu.VMEM((groups - 1, rows, width), f32),
            pltpu.VMEM((2, 8, rows), f32),
            pltpu.VMEM((2, rows, width), bf16),
            pltpu.VMEM((8, rows), f32),
            pltpu.VMEM((groups, 8, rows), f32),
            pltpu.VMEM((STOPS, rows, width), bf16),
            pltpu.VMEM((STOPS, rows, width), bf16),
            pltpu.VMEM((8, rows), f32),
            pltpu.VMEM((loops, 8, rows), f32),
            pltpu.VMEM((groups, table_rows, rows), f32),
            pltpu.VMEM((STOPS * rows, rows), f32),
            pltpu.VMEM(((STOPS - 1) * rows, width), bf16),
            pltpu.VMEM(((STOPS - 1) * rows, width), bf16),
            pltpu.VMEM((STOPS - 1, rows, width), f32),
            pltpu.VMEM((groups * rows, width), bf16),
            pltpu.VMEM((groups * rows, width), bf16),
            pltpu.VMEM((table_rows, groups * rows), bf16),
            pltpu.VMEM((8, rows), f32),
            pltpu.SemaphoreType.DMA((10, max(groups, STOPS) + 1)),
            pltpu.SemaphoreType.DMA((10, max(groups, STOPS) + 1)),
            pltpu.SemaphoreType.DMA((loops,)),
            pltpu.SemaphoreType.DMA((loops,)),
            pltpu.SemaphoreType.DMA((3,)),
            pltpu.SemaphoreType.DMA((3,)),
        ],
        compiler_params=pltpu.CompilerParams(
            collective_id=0, has_side_effects=True, vmem_limit_bytes=60 * 1024 * 1024
        ),
    )(queries, passages, hard_table, index)
    done = pl.pallas_call(
        hand_over,
        out_shape=tuple(jax.ShapeDtypeStruct(x.shape, x.dtype) for x in out[1:]),
        in_specs=[anywhere] * 3,
        out_specs=(anywhere,) * 3,
        scratch_shapes=[pltpu.VMEM(x.shape, x.dtype) for x in out[1:]]
        + [pltpu.SemaphoreType.DMA((12,)), pltpu.SemaphoreType.DMA((12,))],
        compiler_params=pltpu.CompilerParams(vmem_limit_bytes=60 * 1024 * 1024),
    )(*out[1:])
    return (out[0].reshape(()),) + tuple(done)


def solution(mesh):
    rows = P(("blk", "grp"), None)
    return jax.shard_map(
        functools.partial(local, mesh.shape["blk"], mesh.shape["grp"]),
        mesh=mesh,
        in_specs=(rows, rows, rows, rows),
        out_specs=(P(), rows, rows, rows),
        check_vma=False,
    )
```

```python
import functools

import jax
import jax.numpy as jnp
from jax import lax
from jax.experimental import pallas as pl
from jax.experimental.pallas import tpu as pltpu
from jax.sharding import PartitionSpec as P

STOPS = 4
SCALE = 0.015625
TOP = 32766.0
LOW = -1e30
MESH = pl.DeviceIdType.MESH
HIGHEST = lax.Precision.HIGHEST

QUERY, QUERY_META, PASSAGE, PASSAGE_META, STATS, PARTIAL, LSE, GRAD, MERGE, MERGE_META = range(10)


def as_column(row, count):
    return jnp.broadcast_to(row, (128, count)).T[:, 0:1]


def as_row(column, count):
    return jnp.broadcast_to(column, (count, 128)).T[0:1, :]


def coded(value):
    largest = jnp.max(jnp.abs(value), axis=1, keepdims=True)
    largest = jnp.maximum(largest, 1e-30)
    code = jnp.round(value * (TOP / largest)).astype(jnp.int32).astype(jnp.int16)
    return code, largest * (1.0 / TOP)


def halves(code):
    value = code.astype(jnp.int32).astype(jnp.float32)
    high = value.astype(jnp.bfloat16)
    return high, (value - high.astype(jnp.float32)).astype(jnp.bfloat16)


def two_terms(value):
    high = value.astype(jnp.bfloat16)
    return high, (value - high.astype(jnp.float32)).astype(jnp.bfloat16)


def mm(a, b):
    return jnp.dot(a, b, preferred_element_type=jnp.float32)


def nt(a, b, precision=None):
    return lax.dot_general(
        a, b, (((1,), (1,)), ((), ())), precision=precision, preferred_element_type=jnp.float32
    )


def kernel(
    loops, groups,
    q_hbm, p_hbm, t_hbm, idx_ref,
    loss_ref, qg_out, pg_out, tg_out,
    q_ref, p_ref, t_ref, qg_ref, pg_ref, tg_ref, q16, qmeta, p16, pmeta, st_send, st_recv, a_send, a_recv, af, m_stat, m_recv, lse_send, lse_recv,
    g_send, g_recv, l_send, l_recv, ch, sw, phi, plo, gf, qhi, qlo, whi, w_top,
    send_sem, recv_sem, lsend_sem, lrecv_sem, load_sem, save_sem,
):
    b = lax.axis_index("blk")
    g = lax.axis_index("grp")
    rows, width = q_ref.shape
    table_rows = t_ref.shape[0]
    loads = [
        pltpu.make_async_copy(src, dst, load_sem.at[i])
        for i, (src, dst) in enumerate(((q_hbm, q_ref), (p_hbm, p_ref), (t_hbm, t_ref)))
    ]
    for load in loads:
        load.start()
    barrier = pltpu.get_barrier_semaphore()
    for j in range(1, groups):
        pl.semaphore_signal(
            barrier, inc=1, device_id=(b, lax.rem(g + j, groups)), device_id_type=MESH
        )

    def greet(k, carry):
        pl.semaphore_signal(
            barrier, inc=1, device_id=(lax.rem(b + k, loops), g), device_id_type=MESH
        )
        return carry

    lax.fori_loop(1, loops, greet, 0)

    def copy(kind, j, src, dst, device, slot=None):
        return pltpu.make_async_remote_copy(
            src_ref=src,
            dst_ref=dst,
            send_sem=send_sem.at[kind, j],
            recv_sem=recv_sem.at[kind, j if slot is None else slot],
            device_id=device,
            device_id_type=MESH,
        )

    copies = {}

    def go(kind, j, src, dst, device, slot=None):
        copies[kind, j] = copy(kind, j, src, dst, device, slot)
        copies[kind, j].start()

    def arrived(kind, slot, ref):
        copy(kind, 0, ref, ref, (b, lax.rem(g + 1, groups)), slot).wait_recv()

    assert groups == 4
    half = g // 2
    inner = lax.rem(g, 2) == 1 - half
    near = inner.astype(jnp.int32)
    others = [None, g + 1 - 2 * lax.rem(g, 2), 2 - half, 3 - 3 * half]

    own_right = copy(QUERY, 0, q16.at[g], q16.at[g], (b, jnp.minimum(g + 1, groups - 1)), g)
    own_left = copy(QUERY, groups, q16.at[g], q16.at[g], (b, jnp.maximum(g - 1, 0)), g)

    def onward(j):
        src = others[j]
        step = jnp.where(src < g, 1, -1)
        dst = g + step
        return (dst >= 0) & (dst < groups), copy(
            QUERY, j, q16.at[src], q16.at[src], (b, jnp.clip(dst, 0, groups - 1)), src
        )

    def receive(j):
        src = others[j]
        arrived(QUERY, src, q16.at[src])
        valid, forward = onward(j)

        @pl.when(valid)
        def _():
            forward.start()

    loads[0].wait()
    query = q_ref[...]
    code, scale = coded(query)
    q16[g] = code
    qmeta[g, 0:8, :] = idx_ref[...].astype(jnp.float32)
    qmeta[g, 8:16, :] = jnp.broadcast_to(as_row(scale, rows), (8, rows))
    pl.semaphore_wait(barrier, groups - 1 + loops - 1)

    @pl.when(g < groups - 1)
    def _():
        own_right.start()

    @pl.when(g > 0)
    def _():
        own_left.start()

    for j in range(1, groups):
        go(QUERY_META, j, qmeta.at[g], qmeta.at[g], (b, others[j]), g)
    loads[1].wait()
    code, scale = coded(p_ref[...])
    p16[0] = code
    pmeta[0] = jnp.broadcast_to(as_row(scale, rows), (8, rows))
    for s in range(1, STOPS):
        go(PASSAGE_META, s, pmeta.at[0], pmeta.at[s], (lax.rem(b + s, loops), g))
    for s in (3, 1):
        go(PASSAGE, s, p16.at[0], p16.at[s], (lax.rem(b + s, loops), g))
    loads[2].wait()

    row_id = lax.broadcasted_iota(jnp.int32, (table_rows, rows), 0).astype(jnp.float32) + (
        g * table_rows
    ).astype(jnp.float32)

    def count(j):
        src = g if j == 0 else others[j]
        named = jnp.zeros((table_rows, rows), jnp.float32)
        for k in range(8):
            named = named + jnp.where(row_id == qmeta[src, k:k + 1, :], 1.0, 0.0)
        ch[j] = named

    def hard_part(j):
        src = g if j == 0 else others[j]
        high, low = halves(q16[src])
        qhi[j * rows:(j + 1) * rows, :] = high
        qlo[j * rows:(j + 1) * rows, :] = low
        table = t_ref[...]
        both = nt(table, jnp.concatenate([high, low], axis=0))
        scores = (both[:, 0:rows] + both[:, rows:]) * (qmeta[src, 8:9, :] * SCALE)
        named = ch[j]
        top = jnp.max(jnp.where(named > 0.0, scores, LOW), axis=0, keepdims=True)
        part = named * jnp.exp(jnp.minimum(scores - top, 0.0))
        ch[j] = part
        st_send[j, 0:1, :] = top
        st_send[j, 1:2, :] = jnp.sum(part, axis=0, keepdims=True)
        if j > 0:
            go(STATS, j, st_send.at[j], st_recv.at[g], (b, src), g)
        partial = mm(part.T.astype(jnp.bfloat16), table)
        if j == 0:
            af[0] = partial
        elif j == 1:
            a_send[j] = partial.astype(jnp.bfloat16)
            go(PARTIAL, j, a_send.at[j], a_recv.at[0], (b, src), 0)
        else:
            af[j - 1] = partial

            @pl.when(jnp.logical_not(inner))
            def _():
                a_send[j] = partial.astype(jnp.bfloat16)
                merge_stats(j).start()
                merge_block(j).start()

    def merge_stats(j):
        return copy(MERGE_META, j, st_send.at[j], m_stat.at[j - 2], (b, others[1]))

    def merge_block(j):
        return copy(MERGE, j, a_send.at[j], m_recv.at[j - 2], (b, others[1]))

    def joined_block(j):
        return copy(PARTIAL, j, a_send.at[j], a_recv.at[1], (b, others[j]), 1)

    def join(j):
        @pl.when(inner)
        def _():
            merge_stats(j).wait_recv()
            merge_block(j).wait_recv()
            here, there = st_send[j, 0:1, :], m_stat[j - 2, 0:1, :]
            most = jnp.maximum(here, there)
            a_send[j] = (
                af[j - 1] * as_column(jnp.exp(here - most), rows)
                + m_recv[j - 2].astype(jnp.float32) * as_column(jnp.exp(there - most), rows)
            ).astype(jnp.bfloat16)
            joined_block(j).start()

    def window_part(s):
        if s == 0:
            sw[0:rows, :] = nt(p_ref[...], query, HIGHEST) * SCALE
            return
        high, low = halves(p16[s])
        at = slice((s - 1) * rows, s * rows)
        phi[at, :] = high
        plo[at, :] = low
        own_high, own_low = qhi[0:rows, :], qlo[0:rows, :]
        both = nt(high, jnp.concatenate([own_high, own_low], axis=0))
        scores = both[:, 0:rows] + both[:, rows:] + nt(low, own_high)
        sw[s * rows:(s + 1) * rows, :] = (
            scores * as_column(pmeta[s, 0:1, :], rows) * (qmeta[g, 8:9, :] * SCALE)
        )

    def window_grad():
        top = jnp.max(sw[...], axis=0, keepdims=True)
        sw[...] = jnp.exp(sw[...] - top)
        w_top[...] = jnp.broadcast_to(top, (8, rows))
        high, low = two_terms(
            jnp.concatenate(
                [
                    sw[s * rows:(s + 1) * rows, :] * as_column(pmeta[s, 0:1, :], rows)
                    for s in range(1, STOPS)
                ],
                axis=0,
            ).T
        )
        qg_ref[...] = jnp.dot(
            sw[0:rows, :].T, p_ref[...], precision=HIGHEST, preferred_element_type=jnp.float32
        ) + (mm(high, phi[...]) + mm(low, phi[...]) + mm(high, plo[...]))

    st_send[...] = jnp.zeros_like(st_send)
    count(0)
    hard_part(0)
    window_part(0)
    for j in range(1, groups):
        arrived(QUERY_META, others[j], qmeta.at[others[j]])
        count(j)
    positive = jnp.sum(query * p_ref[...]) * SCALE
    def window_next(s):
        copies[PASSAGE_META, s].wait_recv()
        if s == 2:
            copies[PASSAGE, s].wait_recv()
        window_part(s)

    receive(1)
    if groups > 2:

        @pl.when(near > 0)
        def _():
            receive(2)

    hard_part(1)
    if groups > 2:

        @pl.when(near == 0)
        def _():
            receive(2)

    odd = lax.rem(b, 2)
    partner = b + 1 - 2 * odd
    for s in (1, 3):
        copies[PASSAGE, s].wait_recv()
    go(PASSAGE, 2, p16.at[1 + 2 * odd], p16.at[2], (partner, g))
    window_next(1)

    @pl.when(near > 0)
    def _():
        receive(3)

    hard_part(2)

    for s in range(2, STOPS):
        window_next(s)

    @pl.when(near == 0)
    def _():
        window_grad()
        receive(3)

    hard_part(3)

    @pl.when(near > 0)
    def _():
        window_grad()

    join(2)

    tops = [w_top[0:1, :], st_send[0, 0:1, :]]
    for j in range(1, groups):
        arrived(STATS, others[j], st_recv.at[others[j]])
        tops.append(st_recv[others[j], 0:1, :])
    top = functools.reduce(jnp.maximum, tops)
    total = jnp.sum(sw[...], axis=0, keepdims=True) * jnp.exp(tops[0] - top)
    total = total + st_send[0, 1:2, :] * jnp.exp(tops[1] - top)
    for j in range(1, groups):
        total = total + st_recv[others[j], 1:2, :] * jnp.exp(tops[j + 1] - top)
    lse = top + jnp.log(total)
    lse_send[0:1, :] = lse
    lse_send[1:8, :] = jnp.broadcast_to(jnp.sum(lse) - positive, (7, rows))
    for j in range(1, groups):
        go(LSE, j, lse_send, lse_recv.at[g], (b, others[j]), g)

    sw[...] = sw[...] * jnp.exp(tops[0] - lse)
    whi_, wlo_ = two_terms(sw[rows:, :] * qmeta[g, 8:9, :])
    terms = mm(
        jnp.concatenate([whi_, whi_], axis=1),
        jnp.concatenate([qhi[0:rows, :], qlo[0:rows, :]], axis=0),
    ) + mm(wlo_, qhi[0:rows, :])
    alone, joined = 3 - 2 * odd, 1 + 2 * odd
    for s in range(1, STOPS):
        term = terms[(s - 1) * rows:s * rows, :]
        gf[s - 1] = term
        g_send[s - 1] = term.astype(jnp.bfloat16)
    go(GRAD, 0, g_send.at[1], g_recv.at[0], (partner, g))
    go(GRAD, 1, g_send.at[alone - 1], g_recv.at[1], (lax.rem(b + loops - alone, loops), g))
    pg_ref[...] = jnp.dot(
        sw[0:rows, :], query, precision=HIGHEST, preferred_element_type=jnp.float32
    )

    copies[GRAD, 0].wait_recv()
    g_send[STOPS - 1] = (gf[joined - 1] + g_recv[0].astype(jnp.float32)).astype(jnp.bfloat16)
    go(GRAD, 2, g_send.at[STOPS - 1], g_recv.at[2], (lax.rem(b + loops - joined, loops), g))
    group_loss = lse_send[1:2, :]
    whi[:, 0:rows] = (
        ch[0] * (jnp.exp(tops[1] - lse) * (qmeta[g, 8:9, :] * SCALE))
    ).astype(jnp.bfloat16)
    for j in range(1, groups):
        src = others[j]
        arrived(LSE, src, lse_recv.at[src])
        group_loss = group_loss + lse_recv[src, 1:2, :]
        factor = jnp.exp(jnp.minimum(st_send[j, 0:1, :] - lse_recv[src, 0:1, :], 0.0))
        whi[:, j * rows:(j + 1) * rows] = (
            ch[j] * (factor * (qmeta[src, 8:9, :] * SCALE))
        ).astype(jnp.bfloat16)

    l_send[...] = jnp.broadcast_to(group_loss, (8, rows))
    l_recv[0] = jnp.broadcast_to(group_loss, (8, rows))

    def loss_copy(k):
        return pltpu.make_async_remote_copy(
            src_ref=l_send,
            dst_ref=l_recv.at[k],
            send_sem=lsend_sem.at[k],
            recv_sem=lrecv_sem.at[k],
            device_id=(lax.rem(b + k, loops), g),
            device_id_type=MESH,
        )

    def loss_start(k, carry):
        loss_copy(k).start()
        return carry

    lax.fori_loop(1, loops, loss_start, 0)
    join(3)

    tile = 256

    def table_tile(step, carry):
        cols = pl.ds(pl.multiple_of(step * tile, tile), tile)
        left = whi[...]
        tg_ref[:, cols] = (
            jnp.dot(left, qhi[:, cols], preferred_element_type=jnp.float32)
            + jnp.dot(left, qlo[:, cols], preferred_element_type=jnp.float32)
        ).astype(jnp.bfloat16)
        return carry

    lax.fori_loop(0, width // tile, table_tile, 0)
    saves = [
        pltpu.make_async_copy(src, dst, save_sem.at[i])
        for i, (src, dst) in enumerate(((tg_ref, tg_out), (qg_ref, qg_out), (pg_ref, pg_out)))
    ]
    saves[0].start()

    qg_ref[...] = (
        qg_ref[...] * as_column(jnp.exp(tops[0] - lse), rows)
        + af[0] * as_column(jnp.exp(tops[1] - lse), rows)
        - p_ref[...]
    )
    arrived(PARTIAL, 0, a_recv.at[0])
    parts = a_recv[0].astype(jnp.float32) * as_column(jnp.exp(tops[2] - lse), rows)
    arrived(PARTIAL, 1, a_recv.at[1])
    parts = parts + a_recv[1].astype(jnp.float32) * as_column(
        jnp.exp(jnp.maximum(tops[3], tops[4]) - lse), rows
    )
    qg_ref[...] = (qg_ref[...] + parts) * SCALE
    saves[1].start()
    sums = pg_ref[...]
    for s in range(1, 3):
        copies[GRAD, s].wait_recv()
        sums = sums + g_recv[s].astype(jnp.float32)
    pg_ref[...] = (sums - query) * SCALE
    saves[2].start()

    def loss_wait(k, carry):
        loss_copy(k).wait()
        return carry

    lax.fori_loop(1, loops, loss_wait, 0)
    loss_ref[0, 0] = jnp.sum(l_recv[:, 0:1, 0:1]) / (rows * loops * groups)
    for each in copies.values():
        each.wait_send()

    for j in range(2, groups):

        @pl.when(inner)
        def _():
            joined_block(j).wait_send()

        @pl.when(jnp.logical_not(inner))
        def _():
            merge_stats(j).wait_send()
            merge_block(j).wait_send()

    @pl.when(g < groups - 1)
    def _():
        own_right.wait_send()

    @pl.when(g > 0)
    def _():
        own_left.wait_send()

    for j in range(1, groups):
        valid, forward = onward(j)

        @pl.when(valid)
        def _():
            forward.wait_send()

    for save in saves:
        save.wait()


def hand_over(a_ref, b_ref, c_ref, a_out, b_out, c_out, a_here, b_here, c_here, sem_in, sem_out):
    trips = []
    for src, here, dst in ((c_ref, c_here, c_out), (a_ref, a_here, a_out), (b_ref, b_here, b_out)):
        part = src.shape[0] // 4
        for i in range(4):
            at, k = pl.ds(i * part, part), len(trips)
            trips.append((
                pltpu.make_async_copy(src.at[at], here.at[at], sem_in.at[k]),
                pltpu.make_async_copy(here.at[at], dst.at[at], sem_out.at[k]),
            ))
    for bring, _ in trips:
        bring.start()
    for bring, store in trips:
        bring.wait()
        store.start()
    for _, store in trips:
        store.wait()


def local(loops, groups, queries, passages, hard_table, hard_index):
    rows, width = queries.shape
    table_rows = hard_table.shape[0]
    index = hard_index.T
    anywhere = pl.BlockSpec(memory_space=pl.ANY)
    vmem = pl.BlockSpec(memory_space=pltpu.VMEM)
    f32, bf16, i16 = jnp.float32, jnp.bfloat16, jnp.int16
    out = pl.pallas_call(
        functools.partial(kernel, loops, groups),
        out_shape=(
            jax.ShapeDtypeStruct((1, 1), f32),
            jax.ShapeDtypeStruct((rows, width), f32),
            jax.ShapeDtypeStruct((rows, width), f32),
            jax.ShapeDtypeStruct((table_rows, width), bf16),
        ),
        in_specs=[anywhere] * 3 + [vmem],
        out_specs=(pl.BlockSpec(memory_space=pltpu.SMEM),) + (anywhere,) * 3,
        scratch_shapes=[
            pltpu.VMEM((rows, width), f32),
            pltpu.VMEM((rows, width), f32),
            pltpu.VMEM((table_rows, width), bf16),
            pltpu.VMEM((rows, width), f32),
            pltpu.VMEM((rows, width), f32),
            pltpu.VMEM((table_rows, width), bf16),
            pltpu.VMEM((groups, rows, width), i16),
            pltpu.VMEM((groups, 16, rows), f32),
            pltpu.VMEM((STOPS, rows, width), i16),
            pltpu.VMEM((STOPS, 8, rows), f32),
            pltpu.VMEM((groups, 8, rows), f32),
            pltpu.VMEM((groups, 8, rows), f32),
            pltpu.VMEM((groups, rows, width), bf16),
            pltpu.VMEM((2, rows, width), bf16),
            pltpu.VMEM((groups - 1, rows, width), f32),
            pltpu.VMEM((2, 8, rows), f32),
            pltpu.VMEM((2, rows, width), bf16),
            pltpu.VMEM((8, rows), f32),
            pltpu.VMEM((groups, 8, rows), f32),
            pltpu.VMEM((STOPS, rows, width), bf16),
            pltpu.VMEM((STOPS, rows, width), bf16),
            pltpu.VMEM((8, rows), f32),
            pltpu.VMEM((loops, 8, rows), f32),
            pltpu.VMEM((groups, table_rows, rows), f32),
            pltpu.VMEM((STOPS * rows, rows), f32),
            pltpu.VMEM(((STOPS - 1) * rows, width), bf16),
            pltpu.VMEM(((STOPS - 1) * rows, width), bf16),
            pltpu.VMEM((STOPS - 1, rows, width), f32),
            pltpu.VMEM((groups * rows, width), bf16),
            pltpu.VMEM((groups * rows, width), bf16),
            pltpu.VMEM((table_rows, groups * rows), bf16),
            pltpu.VMEM((8, rows), f32),
            pltpu.SemaphoreType.DMA((10, max(groups, STOPS) + 1)),
            pltpu.SemaphoreType.DMA((10, max(groups, STOPS) + 1)),
            pltpu.SemaphoreType.DMA((loops,)),
            pltpu.SemaphoreType.DMA((loops,)),
            pltpu.SemaphoreType.DMA((3,)),
            pltpu.SemaphoreType.DMA((3,)),
        ],
        compiler_params=pltpu.CompilerParams(
            collective_id=0, has_side_effects=True, vmem_limit_bytes=60 * 1024 * 1024
        ),
    )(queries, passages, hard_table, index)
    done = pl.pallas_call(
        hand_over,
        out_shape=tuple(jax.ShapeDtypeStruct(x.shape, x.dtype) for x in out[1:]),
        in_specs=[anywhere] * 3,
        out_specs=(anywhere,) * 3,
        scratch_shapes=[pltpu.VMEM(x.shape, x.dtype) for x in out[1:]]
        + [pltpu.SemaphoreType.DMA((12,)), pltpu.SemaphoreType.DMA((12,))],
        compiler_params=pltpu.CompilerParams(vmem_limit_bytes=60 * 1024 * 1024),
    )(*out[1:])
    return (out[0].reshape(()),) + tuple(done)


def solution(mesh):
    rows = P(("blk", "grp"), None)
    return jax.shard_map(
        functools.partial(local, mesh.shape["blk"], mesh.shape["grp"]),
        mesh=mesh,
        in_specs=(rows, rows, rows, rows),
        out_specs=(P(), rows, rows, rows),
        check_vma=False,
    )
```
